128 devices in a mesh: seq: 4 (over x_lo, core), mp: 32 (over z, x_hi, y).
Axes of the slice: x: 4 (x_hi: 2, x_lo: 2; x = x_hi * 2 + x_lo), y: 4, z: 4, core: 2. Of those that a mesh axis runs over, the one named last changes fastest.
Arguments:
- next_ids: int32 [4096], P('seq'), may hold values from 0 to 64639
- hidden: bfloat16 [4096, 7168], P('seq', 'mp')
- table: bfloat16 [64640, 7168], P('seq', 'mp')
- gain_hidden: float32 [7168], P('mp'), may hold values from 0.1 to 1.9
- gain_embed: float32 [7168], P('mp'), may hold values from 0.1 to 1.9
- proj_weight: bfloat16 [2, 7168, 7168], P(None, 'mp')
- gain_attn: float32 [7168], replicated, may hold values from 0.1 to 1.9
- latent_weight: bfloat16 [7168, 2112], P('mp'), may hold values from -0.0625 to 0.0625
- gain_query: float32 [1536], replicated, may hold values from 0.1 to 1.9
- gain_kv: float32 [512], replicated, may hold values from 0.1 to 1.9
- query_weight: bfloat16 [1536, 24576], P(None, 'mp'), may hold values from -0.15625 to 0.15625
Outputs:
- queries: bfloat16 [4096, 24576], P('seq', 'mp')
- kv_latent: bfloat16 [4096, 512], P('seq')
- key_rope: bfloat16 [4096, 64], P('seq')
The draws below stay inside these ranges and needn't reach their ends.
All inputs are finite; a program needn't handle non-finite values.
Results may differ from the reference program's by a relative error of at most 0.034.
Values may be sent and summed in bfloat16 or wider, within the bound.
No kernel may reach another device: no remote copies, remote signals or barrier semaphores. Data moves between devices by JAX's collectives and lax.ppermute only.
A program may use at most 192 MiB of HBM per device.

```python
import math
import jax
import jax.numpy as jnp
import numpy as np
from jax import lax

D = 7168
VOCAB = 64640
QL = 1536
KVL = 512
ROPE = 64
NOPE = 128
HEADS = 128
TOKENS = 4096
N_MP = 32


def scaled_field(base, key, ramp, row_spread):
    row_key, column_key = jax.random.split(key)
    row_total = base.shape[0]
    column_total = base.shape[1]
    row_scale = jnp.exp(jax.random.uniform(row_key, (row_total, 1)) * math.log(row_spread))
    position = jnp.arange(column_total, dtype=jnp.float32)[None, :] / column_total
    column_scale = jnp.power(ramp, position) * jnp.exp(jax.random.uniform(column_key, (1, column_total)) * math.log(3.0))
    return base * row_scale * column_scale * 0.25


def draw_hidden(key, part):
    key = jax.random.fold_in(key, 11)
    base_key, scale_key = jax.random.split(key, 2)
    base = jax.random.normal(base_key, (TOKENS, D))
    return scaled_field(base, scale_key, 2.0, 10.0).astype(jnp.bfloat16)


def draw_table(key, part):
    key = jax.random.fold_in(key, 23)
    base_key, scale_key = jax.random.split(key, 2)
    base = jax.random.normal(base_key, (VOCAB, D))
    return scaled_field(base, scale_key, 2.0, 10.0).astype(jnp.bfloat16)


def ramped_weight(base, key, ramp):
    column_key, pair_key = jax.random.split(key)
    position = jnp.arange(D, dtype=jnp.float32) / D
    column_scale = jnp.power(ramp, position) * jnp.exp(jax.random.uniform(column_key, (D,)) * math.log(2.0))
    column_scale = column_scale / jnp.sqrt(jnp.mean(column_scale * column_scale))
    block_width = D // N_MP
    block_index = jnp.arange(D, dtype=jnp.int32) // block_width
    pairing = jax.random.permutation(pair_key, N_MP)
    hit = pairing[block_index][:, None] == block_index[None, :]
    spike = jnp.where(hit, 3.0, 1.0)
    return base * spike[None, :, :] * column_scale[None, None, :] * (2.0 * D) ** (-0.5)


def draw_proj_weight(key, part):
    key = jax.random.fold_in(key, 37)
    base_key, scale_key = jax.random.split(key)
    base = jax.random.normal(base_key, (2, D, D))
    return ramped_weight(base, scale_key, 6.0).astype(jnp.bfloat16)


def place_ends(values, stream_key, low, high):
    index_at = [jax.random.randint(jax.random.fold_in(stream_key, axis), (), 0, length) for axis, length in enumerate(values.shape)]
    main_axis = values.shape.index(max(values.shape))
    neighbour = index_at[:main_axis] + [(index_at[main_axis] + 1) % values.shape[main_axis]] + index_at[main_axis + 1:]
    return values.at[tuple(index_at)].set(low).at[tuple(neighbour)].set(high)


def shard_levels(rng, shape, cuts, low, largest):
    factor_of, own = 1.0, jax.random.fold_in(rng, 6)
    for dim, shards_of in cuts:
        heights = jnp.exp(jax.random.uniform(jax.random.fold_in(own, dim), (shards_of,), jnp.float32, low / len(cuts), largest / len(cuts)))
        factor_of = factor_of * jnp.repeat(heights, shape[dim] // shards_of).reshape([-1 if axis == dim else 1 for axis in range(len(shape))])
    return factor_of


def cumulative_ranks(number_of, lean):
    weights = [(1 << 20) // math.isqrt(grade ** lean) + 1 for grade in range(1, number_of + 1)]
    deviation = 1 + sum(weights) // (1 << 30)
    return np.cumsum(np.array([max(1, weight // deviation) for weight in weights]))


def ranked_ids(rng, shape, count, skew):
    table = cumulative_ranks(count, skew)
    lot = jax.random.randint(jax.random.fold_in(rng, 1), shape, 0, int(table[count - 1]))
    standing = jnp.searchsorted(jnp.asarray(table, jnp.int32), lot, side="right")
    return jax.random.permutation(jax.random.fold_in(rng, 2), count)[standing].astype(jnp.int32)


def centred(rng, dims, spread, limit, cuts=(), held_as=jnp.bfloat16):
    result = jax.random.normal(rng, dims, jnp.float32) * spread
    if len(cuts) > 0:
        result = shard_levels(rng, dims, cuts, -0.22, 0.18) * result
    return jnp.clip(result, min=-limit, max=limit).astype(held_as)


def setup_inputs(seed: int = 0) -> dict:
    key_of = jax.random.split(jax.random.key(seed), 12)
    next_ids = place_ends(ranked_ids(key_of[0], (TOKENS,), VOCAB, 2), jax.random.fold_in(key_of[0], 3), 0, VOCAB - 1).astype(jnp.int32)
    hidden = draw_hidden(jax.random.fold_in(key_of[11], 71), 0)
    table = draw_table(jax.random.fold_in(key_of[11], 71), 0)
    gain_hidden = jnp.clip(1.0 + 0.18 * jax.random.normal(key_of[3], (D,), jnp.float32), 0.1, 1.9)
    gain_embed = jnp.clip(1.0 + 0.18 * jax.random.normal(key_of[4], (D,), jnp.float32), 0.1, 1.9)
    proj_weight = draw_proj_weight(jax.random.fold_in(key_of[11], 71), 0)
    gain_attn = jnp.clip(1.0 + 0.18 * jax.random.normal(key_of[6], (D,), jnp.float32), 0.1, 1.9)
    latent_weight = centred(key_of[7], (D, QL + KVL + ROPE), D ** -0.5, 0.0625, ((0, 32),))
    gain_query = jnp.clip(1.0 + 0.18 * jax.random.normal(key_of[8], (QL,), jnp.float32), 0.1, 1.9)
    gain_kv = jnp.clip(1.0 + 0.18 * jax.random.normal(key_of[9], (KVL,), jnp.float32), 0.1, 1.9)
    query_weight = centred(key_of[10], (QL, HEADS * (NOPE + ROPE)), QL ** -0.5, 0.15625, ((1, 32),))
    return {"next_ids": next_ids, "hidden": hidden, "table": table, "gain_hidden": gain_hidden, "gain_embed": gain_embed, "proj_weight": proj_weight, "gain_attn": gain_attn, "latent_weight": latent_weight, "gain_query": gain_query, "gain_kv": gain_kv, "query_weight": query_weight}


EPSILON = 1e-06
THETA = 10000.0

def rms_norm(values, gain):
    values = values.astype(jnp.float32)
    mean_square = lax.optimization_barrier(jnp.mean(values * values, axis=-1, keepdims=True))
    return values * lax.rsqrt(mean_square + EPSILON) * gain.astype(jnp.float32)

def rotate_pairs(values, positions):
    half_width = values.shape[-1] // 2
    exponent = jnp.arange(half_width, dtype=jnp.float32) * (2.0 / values.shape[-1])
    frequency = jnp.power(THETA, -exponent)
    angles = positions.astype(jnp.float32)[..., None] * frequency
    cosine = jnp.cos(angles)
    sine = jnp.sin(angles)
    first_half = values[..., :half_width]
    second_half = values[..., half_width:]
    return jnp.concatenate([first_half * cosine - second_half * sine, second_half * cosine + first_half * sine], axis=-1)

def latent_parts(latent, positions, gain_query, gain_kv):
    query_latent = rms_norm(latent[:, :QL], gain_query).astype(jnp.bfloat16)
    kv_latent = rms_norm(latent[:, QL:QL + KVL], gain_kv).astype(jnp.bfloat16)
    key_rope = rotate_pairs(latent[:, QL + KVL:], positions).astype(jnp.bfloat16)
    return (query_latent, kv_latent, key_rope)

def query_heads(query_latent, query_weight, positions):
    product = jnp.dot(query_latent, query_weight, preferred_element_type=jnp.float32)
    token_count = product.shape[0]
    head_count = product.shape[1] // (NOPE + ROPE)
    product = product.reshape(token_count, head_count, NOPE + ROPE)
    rotated = rotate_pairs(product[..., NOPE:], positions[:, None])
    merged = jnp.concatenate([product[..., :NOPE], rotated], axis=-1)
    return merged.reshape(token_count, head_count * (NOPE + ROPE)).astype(jnp.bfloat16)

def reference(next_ids, hidden, table, gain_hidden, gain_embed, proj_weight, gain_attn, latent_weight, gain_query, gain_kv, query_weight):
    embed = jnp.take(table, next_ids, axis=0)
    normed_hidden = rms_norm(hidden, gain_hidden).astype(jnp.bfloat16)
    normed_embed = rms_norm(embed, gain_embed).astype(jnp.bfloat16)
    width_dev = D // N_MP

    def add_block(running, block_index):
        offset = block_index * width_dev
        hidden_block = lax.dynamic_slice_in_dim(normed_hidden, offset, width_dev, 1)
        embed_block = lax.dynamic_slice_in_dim(normed_embed, offset, width_dev, 1)
        first_weight = lax.dynamic_slice_in_dim(proj_weight[0], offset, width_dev, 0)
        second_weight = lax.dynamic_slice_in_dim(proj_weight[1], offset, width_dev, 0)
        partial_sum = jnp.dot(hidden_block, first_weight, preferred_element_type=jnp.float32)
        partial_sum = partial_sum + jnp.dot(embed_block, second_weight, preferred_element_type=jnp.float32)
        rounded = lax.optimization_barrier(partial_sum.astype(jnp.bfloat16))
        return (running + rounded.astype(jnp.float32), None)
    projected, _ = lax.scan(add_block, jnp.zeros((TOKENS, D), jnp.float32), jnp.arange(N_MP, dtype=jnp.int32))
    attn_input = rms_norm(projected, gain_attn).astype(jnp.bfloat16)
    latent = jnp.dot(attn_input, latent_weight, preferred_element_type=jnp.float32)
    positions = jnp.arange(TOKENS, dtype=jnp.int32)
    query_latent, kv_latent, key_rope = latent_parts(latent, positions, gain_query, gain_kv)
    queries = query_heads(query_latent, query_weight, positions)
    return (queries, kv_latent, key_rope)
```

```python
import functools

import jax
import jax.numpy as jnp
from jax import lax
from jax.experimental import pallas as pl
from jax.experimental.pallas import tpu as pltpu
from jax.sharding import Mesh, PartitionSpec as P

QL = 1536
KVL = 512
ROPE = 64
NOPE = 128
D = 7168
VOCAB_ROWS = 16160
WIDTH = 224
TOK = 1024
HALF = 512
LAT = QL + KVL + ROPE
PACK = 2176
COLS = 1792

EPSILON = 1e-06
THETA = 10000.0

SIZES = {"xlo": 2, "core": 2, "z": 4, "xhi": 2, "y": 4}
NAMES = ("xlo", "core", "z", "xhi", "y")
BF = jnp.bfloat16
F32 = jnp.float32
MIB = 1 << 20

VM = pl.BlockSpec(memory_space=pltpu.VMEM)
SM = pl.BlockSpec(memory_space=pltpu.SMEM)
AN = pl.BlockSpec(memory_space=pl.ANY)


def shift(x, axis, d):
    n = SIZES[axis]
    return lax.ppermute(x, axis, [(i, (i + d) % n) for i in range(n)])


def gather_ring(x, axis):
    return [x, shift(x, axis, -1), shift(x, axis, 2), shift(x, axis, 1)]


def sum_axis(x, axis):
    if SIZES[axis] == 2:
        return x + shift(x, axis, 1)
    p = gather_ring(x, axis)
    return (p[0] + p[2]) + (p[1] + p[3])


def call(kernel, out_shape, args, specs, scratch=(), flops=0, moved=0, limit=48, **more):
    outs = jax.tree.map(lambda s: VM, out_shape)
    return pl.pallas_call(
        kernel,
        out_shape=out_shape,
        in_specs=specs,
        out_specs=more.pop("out_specs", outs),
        scratch_shapes=list(scratch),
        compiler_params=pltpu.CompilerParams(vmem_limit_bytes=limit * MIB),
        cost_estimate=pl.CostEstimate(flops=flops, bytes_accessed=moved, transcendentals=0),
        **more,
    )(*args)


def shape(dims, dtype=BF):
    return jax.ShapeDtypeStruct(dims, dtype)


STEP = 2048
ROWS = -(-VOCAB_ROWS // STEP) * STEP
NONE = ROWS - 8


def turn_kernel(table_t, rows):
    rows[:, :WIDTH] = table_t[...].astype(F32).T
    rows[:, WIDTH:] = jnp.zeros((STEP, 256 - WIDTH), F32)

    @pl.when(pl.program_id(0) == pl.num_programs(0) - 1)
    def _():
        rows[pl.ds(STEP - 8, 8), :] = jnp.zeros((8, 256), F32)


def turn(table_t):
    return pl.pallas_call(
        turn_kernel,
        grid=(ROWS // STEP,),
        in_specs=[pl.BlockSpec((WIDTH, STEP), lambda i: (0, i))],
        out_specs=pl.BlockSpec((STEP, 256), lambda i: (i, 0)),
        out_shape=shape((ROWS, 256), F32),
        compiler_params=pltpu.CompilerParams(vmem_limit_bytes=40 * MIB),
        cost_estimate=pl.CostEstimate(flops=0, bytes_accessed=24 * MIB, transcendentals=0),
    )(table_t)


def pick_kernel(at, rows, out_a, out_b, picked):
    for part, out in enumerate((out_a, out_b)):

        def some(i, _, part=part):
            for j in range(32):
                t = i * 32 + j
                picked[pl.ds(t, 1), :] = rows[pl.ds(at[part * TOK + t], 1), :]
            return 0

        lax.fori_loop(0, TOK // 32, some, 0)
        out[...] = picked[...].astype(BF)


def pick(rows, at):
    return call(
        pick_kernel,
        [shape((TOK, 256))] * 2,
        [at, rows],
        [SM, VM],
        scratch=[pltpu.VMEM((TOK, 256), F32)],
        moved=44 * MIB,
    )


def high_low(total):
    high = total.astype(BF).astype(F32)
    return high, total - high


def hidden_kernel(x_t, gain, out):
    x = x_t[...].astype(F32)
    high, low = high_low(jnp.sum(x * x, axis=0, keepdims=True))
    row = lax.broadcasted_iota(jnp.int32, (256 - WIDTH, TOK), 0)
    tail = jnp.where(row == 0, high, jnp.where(row == 1, low, 0.0))
    out[...] = jnp.concatenate([x * gain[...], tail], axis=0).T.astype(BF)


def embed_kernel(own, near, far, gain, out):
    x = own[...].astype(F32) + near[...].astype(F32) + far[...].astype(F32)
    high, low = high_low(jnp.sum(x * x, axis=1, keepdims=True))
    lane = lax.broadcasted_iota(jnp.int32, x.shape, 1)
    x = x * gain[...]
    out[...] = jnp.where(lane == WIDTH, high, jnp.where(lane == WIDTH + 1, low, x)).astype(BF)


def square_kernel(*refs):
    args, out = refs[:-1], refs[-1]
    lane = lax.broadcasted_iota(jnp.int32, (8, 128), 1)
    take = jnp.where((lane == WIDTH - 128) | (lane == WIDTH - 127), 1.0, 0.0).astype(BF)

    def row(x):
        d = lax.dot_general(take, x, (((1,), (1,)), ((), ())), preferred_element_type=F32)
        return d[0:1]

    for h in range(2):
        a = args[h * 5 : h * 5 + 5]
        for m in range(2):
            parts = [r[pl.ds(m * HALF, HALF), pl.ds(128, 128)] for r in a[:3]]
            parts.append(a[3 + m][:, pl.ds(128, 128)])
            v = [row(p) for p in parts]
            out[pl.ds(h * 2 + m, 1), :] = (v[0] + v[2]) + (v[1] + v[3])


def load_weights(core, m, own, mine, other, wbuf, sems):
    copies = []
    first = pltpu.make_async_copy(own, wbuf.at[0], sems.at[0])
    first.start()
    copies.append(first)
    for i in range(3):
        for mine_here, group in ((True, mine), (False, other)):
            c = pltpu.make_async_copy(group[i], wbuf.at[i + 1], sems.at[i + 1])
            here = (core == m) if mine_here else (core != m)

            @pl.when(here)
            def _(c=c):
                c.start()

        copies.append(c)
    return copies


def hidden_dot_kernel(place, *refs):
    args, outs, (wbuf, sems) = refs[:22], refs[22:24], refs[24:]
    core = place[0]
    copies = []
    for h in range(2):
        a = args[h * 11 : h * 11 + 11]
        copies.append(load_weights(core, 0, a[4], a[5:8], a[8:11], wbuf.at[h], sems.at[h]))
    for h in range(2):
        a = args[h * 11 : h * 11 + 11]
        for c in copies[h]:
            c.wait()
        lhs = [a[0], a[1], a[3], a[2]]
        for j in range(7):
            cols = pl.ds(j * 256, 256)
            acc = None
            for q in range(4):
                d = jnp.dot(lhs[q][pl.ds(0, HALF), pl.ds(0, WIDTH)], wbuf[h, q, :, cols], preferred_element_type=F32)
                acc = d if acc is None else acc + d
            outs[h][:, cols] = acc


def merge_kernel(pieces, place, fac, *refs):
    args, outs, (wbuf, sems) = refs[:24], refs[24:26], refs[26:]
    core = place[0]
    copies = []
    for h in range(2):
        a = args[h * 12 + 1 : h * 12 + 12]
        copies.append(load_weights(core, 1, a[4], a[5:8], a[8:11], wbuf.at[h], sems.at[h]))
    for h in range(2):
        hid = args[h * 12]
        a = args[h * 12 + 1 : h * 12 + 12]
        for c in copies[h]:
            c.wait()
        at_b = place[1 + h]
        for n, k in enumerate(pieces):
            at = pl.multiple_of(((at_b + k) % 4) * 128, 128)
            low = pl.multiple_of(HALF + at, 128)
            lhs = [
                a[0][pl.ds(low, 128), pl.ds(0, WIDTH)],
                a[1][pl.ds(low, 128), pl.ds(0, WIDTH)],
                a[3][pl.ds(at, 128), pl.ds(0, WIDTH)],
                a[2][pl.ds(low, 128), pl.ds(0, WIDTH)],
            ]
            f = fac[pl.ds(pl.multiple_of(h * HALF + at, 128), 128), :]
            for j in range(7):
                cols = pl.ds(j * 256, 256)
                acc = None
                for q in range(4):
                    d = jnp.dot(lhs[q], wbuf[h, q, :, cols], preferred_element_type=F32)
                    acc = d if acc is None else acc + d
                total = hid[pl.ds(at, 128), cols] * f[:, 0:1] + acc * f[:, 1:2]
                outs[h][n, :, cols] = total.astype(outs[h].dtype)


W_SCRATCH = [pltpu.VMEM((2, 4, WIDTH, COLS), BF), pltpu.SemaphoreType.DMA((2, 4))]


def hidden_dot(place, args):
    return call(
        hidden_dot_kernel,
        [shape((HALF, COLS), F32)] * 2,
        [place, *args],
        [SM] + ([VM] * 4 + [AN] * 7) * 2,
        scratch=W_SCRATCH,
        flops=4 * HALF * 896 * COLS,
        moved=13 * MIB,
    )


def merge(pieces, place, fac, args):
    n = len(pieces)
    out = shape((n, 128, COLS), BF if n == 1 else F32)
    return call(
        functools.partial(merge_kernel, pieces),
        [out, out],
        [place, fac, *args],
        [SM, VM] + ([VM] * 5 + [AN] * 7) * 2,
        scratch=W_SCRATCH,
        flops=4 * n * 128 * 896 * COLS,
        moved=10 * MIB,
    )


def join_kernel(rows, q, low, high, t1, t3):
    t1[:rows] = (q[0, :rows] + low[...].astype(F32)).astype(BF)
    t1[rows:] = q[0, rows:].astype(BF)
    t3[:rows] = q[1, :rows].astype(BF)
    t3[rows:] = (q[1, rows:] + high[...].astype(F32)).astype(BF)


def cut_kernel(place, qa, qb, ra1, ra3, rb1, rb3, keep, send):
    xhi = place[0]
    for h, (q, r1, r3) in enumerate(((qa, ra1, ra3), (qb, rb1, rb3))):
        total = q[2] + r1[...].astype(F32) + r3[...].astype(F32)
        keep[h] = jnp.where(xhi == 0, total[:, :896], total[:, 896:])
        send[h] = jnp.where(xhi == 0, total[:, 896:], total[:, :896]).astype(BF)


def split_square(block):
    lane = lax.broadcasted_iota(jnp.int32, block.shape, 1)
    total = jnp.sum(jnp.where((lane == 64) | (lane == 65), block, 0.0), axis=1, keepdims=True)
    high = total.astype(BF).astype(F32)
    block = jnp.where(lane == 64, high, jnp.where(lane == 65, total - high, block))
    return jnp.where(lane > 65, 0.0, block), total


def latent_kernel(place, keep, recv, gain, *refs):
    weights, outs, (wbuf, acc, sems) = refs[:4], refs[4:8], refs[8:]
    core = place[0]
    copies = []
    for h in range(2):
        for k in range(4):
            for s in range(2):
                c_at = core if s == 0 else 1 - core
                row = pl.multiple_of((k * 2 + c_at) * 112, 16)
                c = pltpu.make_async_copy(
                    weights[h * 2 + s].at[pl.ds(k * 112, 112), :],
                    wbuf.at[h, pl.ds(row, 112), :],
                    sems.at[h, k * 2 + s],
                )
                c.start()
                copies.append(c)
    for h in range(2):
        projected = keep[h] + recv[h].astype(F32)
        square = jnp.sum(projected * projected, axis=1, keepdims=True)
        scaled = (projected * gain[h : h + 1, :]).astype(BF)
        for c in copies[h * 8 : h * 8 + 8]:
            c.wait()
        for j in range(8):
            cols = pl.ds(j * 256, 256)
            acc[:, cols] = jnp.dot(scaled, wbuf[h, :, cols], preferred_element_type=F32)
        last = jnp.dot(scaled, wbuf[h, :, pl.ds(2048, 128)], preferred_element_type=F32)
        lane = lax.broadcasted_iota(jnp.int32, last.shape, 1)
        last, _ = split_square(jnp.where(lane < 64, last, jnp.where(lane == 64, square, 0.0)))
        acc[:, pl.ds(2048, 128)] = last
        at_a = place[1 + h]
        for k in (1, 2, 3):
            at = pl.multiple_of(((at_a + k) % 4) * 32, 32)
            outs[h * 2][k - 1] = acc[pl.ds(at, 32), :].astype(BF)
        at = pl.multiple_of(at_a * 32, 32)
        outs[h * 2 + 1][...] = acc[pl.ds(at, 32), :]


def latent_sum_kernel(place, a0, a1, a2, a3, b0, b1, b2, b3, keep, send, acc):
    xhi = place[0]
    for h, (p0, p1, p2, p3) in enumerate(((a0, a1, a2, a3), (b0, b1, b2, b3))):
        total = (p0[...] + p1[...].astype(F32)) + (p2[...].astype(F32) + p3[...].astype(F32))
        acc[:, :2048] = total[:, :2048]
        acc[:, 2048:], _ = split_square(total[:, 2048:])
        keep[h] = acc[pl.ds(pl.multiple_of(xhi * 16, 16), 16), :]
        send[h] = acc[pl.ds(pl.multiple_of((1 - xhi) * 16, 16), 16), :].astype(BF)


def swap_pairs(block):
    lane = lax.broadcasted_iota(jnp.int32, block.shape, 1)
    ahead = pltpu.roll(block, 96, 1)
    behind = pltpu.roll(block, 32, 1)
    return jnp.where(lane % 64 < 32, ahead, behind)


def norm_kernel(place, keep, recv, gain_q, gain_kv, cos, sin, out):
    for h in range(2):
        total = keep[h] + recv[h].astype(F32)
        last, square = split_square(total[:, 2048:])
        total = total[:, :2048] * lax.rsqrt(square / D + EPSILON)
        last = last * lax.rsqrt(square / D + EPSILON)
        q, kv = total[:, :QL], total[:, QL:]
        q = q * lax.rsqrt(jnp.mean(q * q, axis=1, keepdims=True) + EPSILON) * gain_q[...]
        kv = kv * lax.rsqrt(jnp.mean(kv * kv, axis=1, keepdims=True) + EPSILON) * gain_kv[...]
        at = pl.ds(pl.multiple_of(place[h], 16), 16)
        last = last * cos[at, :] + swap_pairs(last) * sin[at, :]
        out[h, :, :QL] = q.astype(BF)
        out[h, :, QL:2048] = kv.astype(BF)
        out[h, :, 2048:] = last.astype(BF)


def query_kernel(place, weight, cos, sin, *refs):
    blocks, (queries, kv, rope, qbuf, rbuf, sems) = refs[:8], refs[8:]
    copies = []
    n = 0
    for kb in range(4):
        for h in range(2):
            x = blocks[h * 4 + kb]
            product = jnp.dot(x[:, :QL], weight[...], preferred_element_type=F32)
            rbuf[n] = x[:, pl.ds(2048, 128)][:, :ROPE]
            at_b, at_a = place[h * 2], place[h * 2 + 1]
            for ka in range(4):
                at = pl.multiple_of(
                    h * HALF + ((at_b + kb) % 4) * 128 + ((at_a + ka) % 4) * 32, 32
                )
                here = slice(ka * 32, ka * 32 + 32)
                p = product[here]
                c, s = cos[pl.ds(at, 32), :], sin[pl.ds(at, 32), :]
                lane = lax.broadcasted_iota(jnp.int32, c.shape, 1)
                for j in range(6):
                    blk = p[:, j * 128 : j * 128 + 128]
                    if j % 3 != 0:
                        turned = blk * c + swap_pairs(blk) * s
                        mine = lane < 64 if j % 3 == 1 else lane >= 64
                        blk = jnp.where(mine, turned, blk)
                    qbuf[n, here, j * 128 : j * 128 + 128] = blk.astype(BF)
                rows = pl.ds(at, 32)
                for i, (src, dst) in enumerate(
                    (
                        (qbuf.at[n, pl.ds(ka * 32, 32), :], queries.at[rows, :]),
                        (x.at[pl.ds(ka * 32, 32), pl.ds(QL, KVL)], kv.at[rows, :]),
                        (rbuf.at[n, pl.ds(ka * 32, 32), :], rope.at[rows, :]),
                    )
                ):
                    cp = pltpu.make_async_copy(src, dst, sems.at[n, ka, i])
                    cp.start()
                    copies.append(cp)
            n += 1
    for cp in copies:
        cp.wait()


def rope_tables(positions):
    lane = jnp.arange(128, dtype=jnp.int32)
    exponent = (lane % 32).astype(F32) * (2.0 / ROPE)
    angles = positions.astype(F32)[:, None] * jnp.power(THETA, -exponent)
    sign = jnp.where(lane % 64 < 32, -1.0, 1.0).astype(F32)
    return jnp.cos(angles), jnp.sin(angles) * sign


def per_device(
    next_ids,
    hidden,
    table,
    gain_hidden,
    gain_embed,
    proj_weight,
    gain_attn,
    latent_weight,
    gain_query,
    gain_kv,
    query_weight,
):
    xlo, core, z, xhi, y = (lax.axis_index(n).astype(jnp.int32) for n in NAMES)
    seq = xlo * 2 + core
    axes = (("y", "z", y, z), ("z", "y", z, y))

    def ints(*v):
        return jnp.stack(v).astype(jnp.int32)

    def weight(m, k, ia):
        return lax.dynamic_slice(proj_weight, (m, 0, ((ia + k) % 4) * COLS), (1, WIDTH, COLS))[0]

    cut = [[weight(core, k, ia) for k in (1, 2, 3)] for _, _, ia, _ in axes]
    own = [[weight(0, 0, ia), weight(1, 0, ia)] for _, _, ia, _ in axes]

    lat_half = lax.dynamic_slice_in_dim(latent_weight, core * 112, 112, 0)
    lat_half = jnp.pad(lat_half, ((0, 0), (0, PACK - LAT)))
    line = [(zz * 4 + yy, yy * 4 + zz) for zz in range(4) for yy in range(4)]

    near_ids = jnp.concatenate([next_ids, shift(next_ids, "core", 1)])
    far_ids = shift(near_ids, "xlo", 1)
    at = jnp.concatenate([far_ids, near_ids]) - seq * VOCAB_ROWS
    at = jnp.where((at >= 0) & (at < VOCAB_ROWS), at, NONE)

    rows, cut, lat_half = lax.optimization_barrier((table.T, cut, lat_half))
    step_3 = [shift(cut[h][0], axes[h][0], 1) for h in range(2)]
    step_1 = [shift(cut[h][2], axes[h][0], -1) for h in range(2)]
    rows = turn(rows)
    keep, send = pick(rows, at[: 2 * TOK])
    embed_near = keep + shift(send, "core", 1)
    embed_near, step_1, step_3, cut, rows, hidden, lat_half = lax.optimization_barrier(
        (embed_near, step_1, step_3, cut, rows, hidden, lat_half)
    )
    lat_turned = lax.ppermute(lat_half, ("z", "y"), line)
    embed_far = shift(embed_near, "xlo", 1)
    step_2 = [shift(cut[h][1], axes[h][0], 2) for h in range(2)]
    keep, send = pick(rows, at[2 * TOK :])
    got = shift(send, "core", 1)
    hidden_g = call(
        hidden_kernel, shape((TOK, 256)), [hidden.T, gain_hidden[:, None]], [VM, VM]
    )
    keep, got, embed_far, step_2, hidden_g, lat_turned = lax.optimization_barrier(
        (keep, got, embed_far, step_2, hidden_g, lat_turned)
    )
    gain = jnp.pad(gain_embed, (0, 256 - WIDTH))[None]
    embed_g = call(embed_kernel, shape((TOK, 256)), [keep, got, embed_far, gain], [VM] * 4)

    block = [
        jnp.concatenate([v[h * HALF : (h + 1) * HALF] for v in (hidden_g, embed_g)])
        for h in range(2)
    ]
    next_1 = [shift(block[h], axes[h][0], -1) for h in range(2)]
    next_3 = [shift(block[h], axes[h][0], 1) for h in range(2)]
    next_1, next_3 = lax.optimization_barrier((next_1, next_3))
    hidden_2 = [shift(next_1[h][:HALF], axes[h][0], -1) for h in range(2)]
    embed_2 = [shift(next_3[h][HALF:], axes[h][0], 1) for h in range(2)]
    hidden_2, embed_2, lat_turned, lat_half = lax.optimization_barrier(
        (hidden_2, embed_2, lat_turned, lat_half)
    )
    lat = [
        lax.all_gather(lat_turned, "z", axis=0, tiled=True),
        lax.all_gather(lat_half, "y", axis=0, tiled=True),
    ]

    args = []
    for h in range(2):
        args += [block[h], next_1[h], next_3[h], hidden_2[h], embed_2[h]]
    squares = call(square_kernel, shape((4, HALF), F32), args, [VM] * 10)
    squares = [squares[:2], squares[2:]]
    squares = [s + shift(s, axes[h][1], 1) for h, s in enumerate(squares)]
    squares = jnp.concatenate(
        [s + shift(s, axes[h][1], 2) for h, s in enumerate(squares)], axis=1
    )
    squares = sum_axis(squares, "xhi")
    factor = lax.rsqrt(squares / D + EPSILON).T

    moved = []
    for h in range(2):
        mine = [step_1[h], step_2[h], step_3[h]]
        moved.append([*mine, *[shift(m, "core", 1) for m in mine]])

    place = ints(core, z, y)
    args = []
    for h in range(2):
        args += [block[h], next_1[h], next_3[h], hidden_2[h], own[h][0], *moved[h]]
    products = hidden_dot(place, args)
    products, factor = lax.optimization_barrier((products, factor))
    args = []
    for h in range(2):
        args += [products[h], block[h], next_1[h], next_3[h], embed_2[h], own[h][1], *moved[h]]
    far = merge((2,), place, factor, args)
    near = merge((1, 3, 0), place, factor, args)
    lat_w = []
    for h in range(2):
        lat_w += [lat[h], shift(lat[h], "core", 1)]
    got = []
    for h, (_, b, _, _) in enumerate(axes):
        low = shift(far[h][0, :64], b, 1)
        high = shift(far[h][0, 64:], b, -1)
        t1, t3 = call(
            functools.partial(join_kernel, 64),
            [shape((128, COLS))] * 2,
            [near[h], low, high],
            [VM] * 3,
        )
        got += [shift(t1, b, 1), shift(t3, b, -1)]
    keep, send = call(
        cut_kernel,
        [shape((2, 128, 896), F32), shape((2, 128, 896))],
        [ints(xhi), *near, *got],
        [SM] + [VM] * 6,
    )
    recv = shift(send, "xhi", 1)

    gains = jnp.stack(
        [lax.dynamic_slice_in_dim(gain_attn, ia * COLS + xhi * 896, 896) for _, _, ia, _ in axes]
    )
    sent = [shape((3, 32, PACK)), shape((32, PACK), F32)]
    parts = call(
        latent_kernel,
        sent + sent,
        [ints(core, y, z), keep, recv, gains, *lat_w],
        [SM, VM, VM, VM] + [AN] * 4,
        scratch=[
            pltpu.VMEM((2, 896, PACK), BF),
            pltpu.VMEM((128, PACK), F32),
            pltpu.SemaphoreType.DMA((2, 8)),
        ],
        flops=4 * 128 * 896 * PACK,
        moved=8 * MIB,
    )
    blocks = []
    for h, (a, _, _, _) in enumerate(axes):
        p = parts[h * 2]
        blocks += [parts[h * 2 + 1], shift(p[0], a, 1), shift(p[1], a, 2), shift(p[2], a, 3)]
    keep, send = call(
        latent_sum_kernel,
        [shape((2, 16, PACK), F32), shape((2, 16, PACK))],
        [ints(xhi), *blocks],
        [SM] + [VM] * 8,
        scratch=[pltpu.VMEM((32, PACK), F32)],
    )
    recv = shift(send, "xhi", 1)
    cos, sin = rope_tables(seq * TOK + jnp.arange(TOK, dtype=jnp.int32))
    done = call(
        norm_kernel,
        shape((2, 16, PACK)),
        [
            ints(z * 128 + y * 32 + xhi * 16, HALF + y * 128 + z * 32 + xhi * 16),
            keep,
            recv,
            gain_query[None],
            gain_kv[None],
            cos,
            sin,
        ],
        [SM] + [VM] * 6,
    )

    other = shift(done, "xhi", 1)
    pair = (jnp.where(xhi == 0, done, other), jnp.where(xhi == 0, other, done))
    pair = jnp.concatenate(pair, axis=1)
    rows = []
    for h, (a, b, _, _) in enumerate(axes):
        near = jnp.concatenate(gather_ring(pair[h], a), axis=0)
        rows += gather_ring(near, b)
    return call(
        query_kernel,
        [shape((TOK, 768)), shape((TOK, KVL)), shape((TOK, ROPE))],
        [ints(z, y, y, z), query_weight, cos, sin, *rows],
        [SM] + [VM] * 11,
        out_specs=[AN] * 3,
        scratch=[
            pltpu.VMEM((8, 128, 768), BF),
            pltpu.VMEM((8, 128, ROPE), BF),
            pltpu.SemaphoreType.DMA((8, 4, 3)),
        ],
        flops=2 * TOK * QL * 768,
        moved=8 * MIB,
    )


def solution(mesh):
    fine = Mesh(mesh.devices.reshape(2, 2, 4, 2, 4), NAMES)
    seq = ("xlo", "core")
    mp = ("z", "xhi", "y")
    placed = (
        P(seq),
        P(seq, mp),
        P(seq, mp),
        P(mp),
        P(mp),
        P(None, mp, None),
        P(),
        P(mp, None),
        P(),
        P(),
        P(None, mp),
    )
    return jax.shard_map(
        per_device,
        mesh=fine,
        in_specs=placed,
        out_specs=(P(seq, mp), P(seq, None), P(seq, None)),
        check_vma=False,
    )
```

```python
import functools

import jax
import jax.numpy as jnp
from jax import lax
from jax.experimental import pallas as pl
from jax.experimental.pallas import tpu as pltpu
from jax.sharding import Mesh, PartitionSpec as P

QL = 1536
KVL = 512
ROPE = 64
NOPE = 128
D = 7168
VOCAB_ROWS = 16160
WIDTH = 224
TOK = 1024
HALF = 512
LAT = QL + KVL + ROPE
PACK = 2176
COLS = 1792

EPSILON = 1e-06
THETA = 10000.0

SIZES = {"xlo": 2, "core": 2, "z": 4, "xhi": 2, "y": 4}
NAMES = ("xlo", "core", "z", "xhi", "y")
BF = jnp.bfloat16
F32 = jnp.float32
MIB = 1 << 20

VM = pl.BlockSpec(memory_space=pltpu.VMEM)
SM = pl.BlockSpec(memory_space=pltpu.SMEM)
AN = pl.BlockSpec(memory_space=pl.ANY)


def shift(x, axis, d):
    n = SIZES[axis]
    return lax.ppermute(x, axis, [(i, (i + d) % n) for i in range(n)])


def gather_ring(x, axis):
    return [x, shift(x, axis, -1), shift(x, axis, 2), shift(x, axis, 1)]


def sum_axis(x, axis):
    if SIZES[axis] == 2:
        return x + shift(x, axis, 1)
    p = gather_ring(x, axis)
    return (p[0] + p[2]) + (p[1] + p[3])


def call(kernel, out_shape, args, specs, scratch=(), flops=0, moved=0, limit=48, **more):
    outs = jax.tree.map(lambda s: VM, out_shape)
    return pl.pallas_call(
        kernel,
        out_shape=out_shape,
        in_specs=specs,
        out_specs=more.pop("out_specs", outs),
        scratch_shapes=list(scratch),
        compiler_params=pltpu.CompilerParams(vmem_limit_bytes=limit * MIB),
        cost_estimate=pl.CostEstimate(flops=flops, bytes_accessed=moved, transcendentals=0),
        **more,
    )(*args)


def shape(dims, dtype=BF):
    return jax.ShapeDtypeStruct(dims, dtype)


STEP = 2048
ROWS = -(-VOCAB_ROWS // STEP) * STEP
NONE = ROWS - 8


def pick_rows(at, rows, picked, outs):
    for part, out in enumerate(outs):

        def some(i, _, part=part):
            for j in range(32):
                t = i * 32 + j
                picked[pl.ds(t, 1), :] = rows[pl.ds(at[part * TOK + t], 1), :]
            return 0

        lax.fori_loop(0, TOK // 32, some, 0)
        out[...] = picked[...].astype(BF)


def turn_kernel(at, table_t, out_a, out_b, kept, rows, picked, sem):
    step = pl.program_id(0)
    here = pl.ds(pl.multiple_of(step * STEP, STEP), STEP)
    rows[here, :WIDTH] = table_t[...].astype(F32).T
    rows[here, WIDTH:] = jnp.zeros((STEP, 256 - WIDTH), F32)

    @pl.when(step == pl.num_programs(0) - 1)
    def _():
        rows[pl.ds(NONE, 8), :] = jnp.zeros((8, 256), F32)
        copy = pltpu.make_async_copy(rows, kept, sem)
        copy.start()
        pick_rows(at, rows, picked, (out_a, out_b))
        copy.wait()


def turn(table_t, at):
    out = shape((TOK, 256))
    return pl.pallas_call(
        turn_kernel,
        grid_spec=pltpu.PrefetchScalarGridSpec(
            num_scalar_prefetch=1,
            grid=(ROWS // STEP,),
            in_specs=[pl.BlockSpec((WIDTH, STEP), lambda i, *_: (0, i))],
            out_specs=[pl.BlockSpec((TOK, 256), lambda i, *_: (0, 0))] * 2 + [AN],
            scratch_shapes=[
                pltpu.VMEM((ROWS, 256), F32),
                pltpu.VMEM((TOK, 256), F32),
                pltpu.SemaphoreType.DMA,
            ],
        ),
        out_shape=[out, out, shape((ROWS, 256), F32)],
        compiler_params=pltpu.CompilerParams(vmem_limit_bytes=56 * MIB),
        cost_estimate=pl.CostEstimate(flops=0, bytes_accessed=80 * MIB, transcendentals=0),
    )(at, table_t)


def pick_kernel(at, rows, out_a, out_b, picked):
    pick_rows(at, rows, picked, (out_a, out_b))


def pick(rows, at):
    return call(
        pick_kernel,
        [shape((TOK, 256))] * 2,
        [at, rows],
        [SM, VM],
        scratch=[pltpu.VMEM((TOK, 256), F32)],
        moved=44 * MIB,
    )


def high_low(total):
    high = total.astype(BF).astype(F32)
    return high, total - high


def hidden_kernel(x_t, gain, out):
    x = x_t[...].astype(F32)
    high, low = high_low(jnp.sum(x * x, axis=0, keepdims=True))
    row = lax.broadcasted_iota(jnp.int32, (256 - WIDTH, TOK), 0)
    tail = jnp.where(row == 0, high, jnp.where(row == 1, low, 0.0))
    out[...] = jnp.concatenate([x * gain[...], tail], axis=0).T.astype(BF)


def embed_kernel(own, near, far, gain, hid, out_a, out_b):
    x = own[...].astype(F32) + near[...].astype(F32) + far[...].astype(F32)
    high, low = high_low(jnp.sum(x * x, axis=1, keepdims=True))
    lane = lax.broadcasted_iota(jnp.int32, x.shape, 1)
    x = x * gain[...]
    x = jnp.where(lane == WIDTH, high, jnp.where(lane == WIDTH + 1, low, x)).astype(BF)
    for h, out in enumerate((out_a, out_b)):
        out[:HALF] = hid[h * HALF : (h + 1) * HALF]
        out[HALF:] = x[h * HALF : (h + 1) * HALF]


def square_kernel(*refs):
    args, out, buf, sems = refs[:10], refs[10], refs[11], refs[12]
    lane = lax.broadcasted_iota(jnp.int32, (8, 128), 1)
    take = jnp.where((lane == WIDTH - 128) | (lane == WIDTH - 127), 1.0, 0.0).astype(BF)
    copies = []
    for i, a in enumerate(args):
        rows = a.shape[0]
        c = pltpu.make_async_copy(
            a.at[:, pl.ds(128, 128)], buf.at[i, pl.ds(0, rows), :], sems.at[i]
        )
        c.start()
        copies.append(c)
    for c in copies:
        c.wait()

    def row(x):
        d = lax.dot_general(take, x, (((1,), (1,)), ((), ())), preferred_element_type=F32)
        return d[0:1]

    for h in range(2):
        for m in range(2):
            v = [row(buf[h * 5 + i, pl.ds(m * HALF, HALF), :]) for i in range(3)]
            v.append(row(buf[h * 5 + 3 + m, pl.ds(0, HALF), :]))
            out[pl.ds(h * 2 + m, 1), :] = (v[0] + v[2]) + (v[1] + v[3])


def cut_weights_kernel(place, w, out_1, out_2, out_3, own, wbuf, blocks, last, sems):
    core, y = place[0], place[1]
    load = pltpu.make_async_copy(w, wbuf, sems.at[0])
    load.start()
    load.wait()

    def cut(m, to, dst):
        for xhi in range(2):
            parts = []
            for z in range(4):
                at = (z * 2 + xhi) * 896 + to * WIDTH
                parts.append(wbuf[m, :, at : at + WIDTH])
            dst[:, xhi * 896 : (xhi + 1) * 896] = jnp.concatenate(parts, axis=1)

    for to in range(4):
        cut(core, to, blocks.at[to])
        pl.when(y == to)(lambda to=to: cut(1 - core, to, last))
    copies = [
        pltpu.make_async_copy(blocks.at[(y + k) % 4], dst, sems.at[k])
        for k, dst in ((1, out_1), (2, out_2), (3, out_3))
    ]
    copies.append(pltpu.make_async_copy(blocks.at[y], own.at[core], sems.at[4]))
    copies.append(pltpu.make_async_copy(last, own.at[1 - core], sems.at[5]))
    for c in copies:
        c.start()
    for c in copies:
        c.wait()


def load_blocks(core, m, ia, a, wbuf, xbuf, sems):
    copies = []

    def start(src, dst, sem, when=None):
        c = pltpu.make_async_copy(src, dst, sem)
        if when is None:
            c.start()
        else:
            pl.when(when)(lambda: c.start())
        return c

    own = a[10].at[m]
    if a[10].shape[2] != COLS:
        own = own.at[:, pl.ds(pl.multiple_of(ia * COLS, 256), COLS)]
    part = pl.ds(m * HALF, HALF)
    for k, src in ((0, a[0].at[part, :]), (1, a[1].at[part, :]), (2, a[3]), (3, a[2].at[part, :])):
        copies.append(start(src, xbuf.at[k], sems.at[k]))
    copies.append(start(own, wbuf.at[0], sems.at[4]))
    for i in range(3):
        start(a[4 + i], wbuf.at[i + 1], sems.at[5 + i], core == m)
        copies.append(start(a[7 + i], wbuf.at[i + 1], sems.at[5 + i], core != m))
    return copies


def hidden_dot_kernel(place, *refs):
    a, out, (wbuf, xbuf, sems) = refs[:11], refs[11], refs[12:]
    for c in load_blocks(place[0], 0, place[1], a, wbuf, xbuf, sems):
        c.wait()
    for j in range(7):
        cols = pl.ds(j * 256, 256)
        acc = None
        for q in range(4):
            d = jnp.dot(xbuf[q, :, :WIDTH], wbuf[q, :, cols], preferred_element_type=F32)
            acc = d if acc is None else acc + d
        out[:, cols] = acc


def merge_kernel(pieces, h, place, fac, hid, *refs):
    a, outs, (wbuf, xbuf, hbuf, sems) = refs[:11], refs[11:-4], refs[-4:]
    copies = load_blocks(place[0], 1, place[1], a, wbuf, xbuf, sems)
    rows = [pl.multiple_of(((place[2] + k) % 4) * 128, 128) for k in pieces]
    for n, at in enumerate(rows):
        c = pltpu.make_async_copy(hid.at[pl.ds(at, 128), :], hbuf.at[n], sems.at[8 + n])
        c.start()
        copies.append(c)
    for c in copies:
        c.wait()
    for n, at in enumerate(rows):
        f = fac[pl.ds(pl.multiple_of(h * HALF + at, 128), 128), :]
        for j in range(7):
            cols = pl.ds(j * 256, 256)
            acc = None
            for q in range(4):
                x = xbuf[q, pl.ds(at, 128), :WIDTH]
                d = jnp.dot(x, wbuf[q, :, cols], preferred_element_type=F32)
                acc = d if acc is None else acc + d
            total = hbuf[n, :, cols] * f[:, 0:1] + acc * f[:, 1:2]
            if len(pieces) == 1:
                outs[0][:, cols] = total[:64].astype(BF)
                outs[1][:, cols] = total[64:].astype(BF)
            else:
                outs[0][n, :, cols] = total


def hidden_dot(place, args):
    return call(
        hidden_dot_kernel,
        shape((HALF, COLS), F32),
        [place, *args],
        [SM] + [AN] * 11,
        scratch=[
            pltpu.VMEM((4, WIDTH, COLS), BF),
            pltpu.VMEM((4, HALF, 256), BF),
            pltpu.SemaphoreType.DMA((8,)),
        ],
        flops=2 * HALF * 896 * COLS,
        moved=20 * MIB,
        limit=60,
    )


def merge(pieces, h, place, fac, args):
    n = len(pieces)
    return call(
        functools.partial(merge_kernel, pieces, h),
        [shape((64, COLS))] * 2 if n == 1 else [shape((n, 128, COLS), F32)],
        [place, fac, *args],
        [SM, VM] + [AN] * 12,
        scratch=[
            pltpu.VMEM((4, WIDTH, COLS), BF),
            pltpu.VMEM((4, HALF, 256), BF),
            pltpu.VMEM((n, 128, COLS), F32),
            pltpu.SemaphoreType.DMA((8 + n,)),
        ],
        flops=2 * n * 128 * 896 * COLS,
        moved=(10 if n == 1 else 20) * MIB,
        limit=60,
    )


def join_kernel(rows, q, low, high, t1, t3):
    t1[:rows] = (q[0, :rows] + low[...].astype(F32)).astype(BF)
    t1[rows:] = q[0, rows:].astype(BF)
    t3[:rows] = q[1, :rows].astype(BF)
    t3[rows:] = (q[1, rows:] + high[...].astype(F32)).astype(BF)


def cut_kernel(place, qa, qb, ra1, ra3, rb1, rb3, keep, send):
    xhi = place[0]
    for h, (q, r1, r3) in enumerate(((qa, ra1, ra3), (qb, rb1, rb3))):
        total = q[2] + r1[...].astype(F32) + r3[...].astype(F32)
        keep[h] = jnp.where(xhi == 0, total[:, :896], total[:, 896:])
        send[h] = jnp.where(xhi == 0, total[:, 896:], total[:, :896]).astype(BF)


def split_square(block):
    lane = lax.broadcasted_iota(jnp.int32, block.shape, 1)
    total = jnp.sum(jnp.where((lane == 64) | (lane == 65), block, 0.0), axis=1, keepdims=True)
    high = total.astype(BF).astype(F32)
    block = jnp.where(lane == 64, high, jnp.where(lane == 65, total - high, block))
    return jnp.where(lane > 65, 0.0, block), total


def latent_kernel(place, keep, recv, gain, *refs):
    weights, outs, (wbuf, acc, sems) = refs[:4], refs[4:12], refs[12:]
    core = place[0]
    copies = []
    for h in range(2):
        for k in range(4):
            for s in range(2):
                c_at = core if s == 0 else 1 - core
                row = pl.multiple_of((k * 2 + c_at) * 112, 16)
                c = pltpu.make_async_copy(
                    weights[h * 2 + s].at[pl.ds(k * 112, 112), :],
                    wbuf.at[h, pl.ds(row, 112), :],
                    sems.at[h, k * 2 + s],
                )
                c.start()
                copies.append(c)
    for h in range(2):
        projected = keep[h] + recv[h].astype(F32)
        square = jnp.sum(projected * projected, axis=1, keepdims=True)
        scaled = (projected * gain[h : h + 1, :]).astype(BF)
        for c in copies[h * 8 : h * 8 + 8]:
            c.wait()
        for j in range(8):
            cols = pl.ds(j * 256, 256)
            acc[:, cols] = jnp.dot(scaled, wbuf[h, :, cols], preferred_element_type=F32)
        last = jnp.dot(scaled, wbuf[h, :, pl.ds(2048, 128)], preferred_element_type=F32)
        lane = lax.broadcasted_iota(jnp.int32, last.shape, 1)
        last, _ = split_square(jnp.where(lane < 64, last, jnp.where(lane == 64, square, 0.0)))
        acc[:, pl.ds(2048, 128)] = last
        at_a = place[1 + h]
        for k in (1, 2, 3):
            at = pl.multiple_of(((at_a + k) % 4) * 32, 32)
            outs[h * 4 + k][...] = acc[pl.ds(at, 32), :].astype(BF)
        at = pl.multiple_of(at_a * 32, 32)
        outs[h * 4][...] = acc[pl.ds(at, 32), :]


def latent_sum_kernel(a0, a1, a2, a3, b0, b1, b2, b3, out):
    for h, (p0, p1, p2, p3) in enumerate(((a0, a1, a2, a3), (b0, b1, b2, b3))):
        total = (p0[...] + p1[...].astype(F32)) + (p2[...].astype(F32) + p3[...].astype(F32))
        out[h, :, :2048] = total[:, :2048].astype(BF)
        last, _ = split_square(total[:, 2048:])
        out[h, :, 2048:] = last.astype(BF)


def swap_pairs(block):
    lane = lax.broadcasted_iota(jnp.int32, block.shape, 1)
    ahead = pltpu.roll(block, 96, 1)
    behind = pltpu.roll(block, 32, 1)
    return jnp.where(lane % 64 < 32, ahead, behind)


def norm_kernel(place, keep, recv, gain_q, gain_kv, cos, sin, out_a, out_b):
    for h, out in enumerate((out_a, out_b)):
        total = keep[h].astype(F32) + recv[h].astype(F32)
        last, square = split_square(total[:, 2048:])
        total = total[:, :2048] * lax.rsqrt(square / D + EPSILON)
        last = last * lax.rsqrt(square / D + EPSILON)
        q, kv = total[:, :QL], total[:, QL:]
        q = q * lax.rsqrt(jnp.mean(q * q, axis=1, keepdims=True) + EPSILON) * gain_q[...]
        kv = kv * lax.rsqrt(jnp.mean(kv * kv, axis=1, keepdims=True) + EPSILON) * gain_kv[...]
        at = pl.ds(pl.multiple_of(place[h], 32), 32)
        last = last * cos[at, :] + swap_pairs(last) * sin[at, :]
        out[:, :QL] = q.astype(BF)
        out[:, QL:2048] = kv.astype(BF)
        out[:, 2048:] = last.astype(BF)


def query_kernel(parts, given, place, weight, cos, sin, *refs):
    n_parts = len(parts)
    blocks, refs = refs[:n_parts], refs[n_parts + given :]
    queries, kv, rope, qbuf, rbuf, sems = refs
    copies = []
    for n, ((h, kb, first, rows), x) in enumerate(zip(parts, blocks)):
        product = jnp.dot(x[:, :QL], weight[...], preferred_element_type=F32)
        rbuf[n, :rows, :] = x[:, pl.ds(2048, 128)][:, :ROPE]
        at_b, at_a = place[h * 2], place[h * 2 + 1]
        for r in range(rows // 32):
            ka = first // 32 + r
            at = pl.multiple_of(
                h * HALF + ((at_b + kb) % 4) * 128 + ((at_a + ka) % 4) * 32, 32
            )
            here = slice(r * 32, r * 32 + 32)
            p = product[here]
            c, s = cos[pl.ds(at, 32), :], sin[pl.ds(at, 32), :]
            lane = lax.broadcasted_iota(jnp.int32, c.shape, 1)
            for j in range(6):
                blk = p[:, j * 128 : j * 128 + 128]
                if j % 3 != 0:
                    turned = blk * c + swap_pairs(blk) * s
                    mine = lane < 64 if j % 3 == 1 else lane >= 64
                    blk = jnp.where(mine, turned, blk)
                qbuf[n, here, j * 128 : j * 128 + 128] = blk.astype(BF)
            to, part = pl.ds(at, 32), pl.ds(r * 32, 32)
            for i, (src, dst) in enumerate(
                (
                    (qbuf.at[n, part, :], queries.at[to, :]),
                    (x.at[part, pl.ds(QL, KVL)], kv.at[to, :]),
                    (rbuf.at[n, part, :], rope.at[to, :]),
                )
            ):
                cp = pltpu.make_async_copy(src, dst, sems.at[n, r, i])
                cp.start()
                copies.append(cp)
    for cp in copies:
        cp.wait()


def query(parts, place, weight, cos, sin, blocks, given=()):
    n = len(parts)
    tokens = sum(p[3] for p in parts)
    return call(
        functools.partial(query_kernel, parts, len(given)),
        [shape((TOK, 768)), shape((TOK, KVL)), shape((TOK, ROPE))],
        [place, weight, cos, sin, *blocks, *given],
        [SM] + [VM] * (3 + n) + [AN] * len(given),
        out_specs=[AN] * 3,
        scratch=[
            pltpu.VMEM((n, 128, 768), BF),
            pltpu.VMEM((n, 128, ROPE), BF),
            pltpu.SemaphoreType.DMA((n, 4, 3)),
        ],
        flops=2 * tokens * QL * 768,
        moved=6 * MIB,
        input_output_aliases={4 + n + i: i for i in range(len(given))},
    )


def rope_tables(positions):
    lane = jnp.arange(128, dtype=jnp.int32)
    exponent = (lane % 32).astype(F32) * (2.0 / ROPE)
    angles = positions.astype(F32)[:, None] * jnp.power(THETA, -exponent)
    sign = jnp.where(lane % 64 < 32, -1.0, 1.0).astype(F32)
    return jnp.cos(angles), jnp.sin(angles) * sign


def per_device(
    next_ids,
    hidden,
    table,
    gain_hidden,
    gain_embed,
    proj_weight,
    gain_attn,
    latent_weight,
    gain_query,
    gain_kv,
    query_weight,
):
    xlo, core, z, xhi, y = (lax.axis_index(n).astype(jnp.int32) for n in NAMES)
    seq = xlo * 2 + core
    axes = (("y", "z", y, z), ("z", "y", z, y))

    def ints(*v):
        return jnp.stack(v).astype(jnp.int32)

    def weight(m, k, ia):
        return lax.dynamic_slice(proj_weight, (m, 0, ((ia + k) % 4) * COLS), (1, WIDTH, COLS))[0]

    *cut_a, own_a = call(
        cut_weights_kernel,
        [shape((WIDTH, COLS))] * 3 + [shape((2, WIDTH, COLS))],
        [ints(core, y), proj_weight],
        [SM, AN],
        out_specs=[AN] * 4,
        scratch=[
            pltpu.VMEM((2, WIDTH, D), BF),
            pltpu.VMEM((4, WIDTH, COLS), BF),
            pltpu.VMEM((WIDTH, COLS), BF),
            pltpu.SemaphoreType.DMA((6,)),
        ],
        moved=12 * MIB,
        limit=60,
    )
    cut = [cut_a, [weight(core, k, z) for k in (1, 2, 3)]]
    own = [own_a, proj_weight]

    lat_half = lax.dynamic_slice_in_dim(latent_weight, core * 112, 112, 0)
    lat_half = jnp.pad(lat_half, ((0, 0), (0, PACK - LAT)))

    near_ids = jnp.concatenate([next_ids, shift(next_ids, "core", 1)])
    far_ids = shift(near_ids, "xlo", 1)
    at = jnp.concatenate([far_ids, near_ids]) - seq * VOCAB_ROWS
    at = jnp.where((at >= 0) & (at < VOCAB_ROWS), at, NONE)

    rows, cut, lat_half = lax.optimization_barrier((table.T, cut, lat_half))
    step_3 = [shift(cut[h][0], axes[h][0], 1) for h in range(2)]
    step_1 = [shift(cut[h][2], axes[h][0], -1) for h in range(2)]
    keep, send, rows = turn(rows, at[: 2 * TOK])
    embed_near = keep + shift(send, "core", 1)
    embed_near, step_1, step_3, cut, rows, hidden, lat_half = lax.optimization_barrier(
        (embed_near, step_1, step_3, cut, rows, hidden, lat_half)
    )
    embed_far = shift(embed_near, "xlo", 1)
    step_2 = [shift(cut[h][1], axes[h][0], 2) for h in range(2)]
    keep, send = pick(rows, at[2 * TOK :])
    keep, send, embed_far, step_1, step_3 = lax.optimization_barrier(
        (keep, send, embed_far, step_1, step_3)
    )
    got = shift(send, "core", 1)
    hidden_g = call(
        hidden_kernel, shape((TOK, 256)), [hidden.T, gain_hidden[:, None]], [VM, VM]
    )
    other_1 = [shift(m, "core", 1) for m in step_1]
    other_3 = [shift(m, "core", 1) for m in step_3]
    keep, got, embed_far, step_2, hidden_g, other_1, other_3 = lax.optimization_barrier(
        (keep, got, embed_far, step_2, hidden_g, other_1, other_3)
    )
    gain = jnp.pad(gain_embed, (0, 256 - WIDTH))[None]
    block = call(
        embed_kernel, [shape((TOK, 256))] * 2, [keep, got, embed_far, gain, hidden_g], [VM] * 5
    )

    next_1 = [shift(block[h], axes[h][0], -1) for h in range(2)]
    next_3 = [shift(block[h], axes[h][0], 1) for h in range(2)]
    next_1, next_3 = lax.optimization_barrier((next_1, next_3))
    hidden_2 = [shift(next_1[h][:HALF], axes[h][0], -1) for h in range(2)]
    embed_2 = [shift(next_3[h][HALF:], axes[h][0], 1) for h in range(2)]
    hidden_2, embed_2, lat_half = lax.optimization_barrier((hidden_2, embed_2, lat_half))
    lat = [lax.all_gather(lat_half, b, axis=0, tiled=True) for _, b, _, _ in axes]
    other_2 = [shift(m, "core", 1) for m in step_2]
    moved = []
    for h in range(2):
        mine, other = [step_1[h], step_2[h], step_3[h]], [other_1[h], other_2[h], other_3[h]]
        moved.append([*mine, *other, own[h]])

    args = []
    for h in range(2):
        args += [block[h], next_1[h], next_3[h], hidden_2[h], embed_2[h]]
    squares = call(
        square_kernel,
        shape((4, HALF), F32),
        args,
        [AN] * 10,
        scratch=[pltpu.VMEM((10, TOK, 128), BF), pltpu.SemaphoreType.DMA((10,))],
        limit=60,
    )
    squares = [squares[:2], squares[2:]]
    products = []
    for step in range(2):
        squares = [s + shift(s, axes[h][1], step + 1) for h, s in enumerate(squares)]
        h = step
        products.append(
            hidden_dot(
                ints(core, axes[h][2]), [block[h], next_1[h], next_3[h], hidden_2[h], *moved[h]]
            )
        )
        squares, products, moved = lax.optimization_barrier((squares, products, moved))
    squares = sum_axis(jnp.concatenate(squares, axis=1), "xhi")
    factor = lax.rsqrt(squares / D + EPSILON).T

    args, places = [], []
    for h, (_, _, ia, ib) in enumerate(axes):
        args.append([products[h], block[h], next_1[h], next_3[h], embed_2[h], *moved[h]])
        places.append(ints(core, ia, ib))
    low, high, near = [], [], []
    for h, (_, b, _, _) in enumerate(axes):
        far = merge((2,), h, places[h], factor, args[h])
        low.append(shift(far[0], b, 1))
        high.append(shift(far[1], b, -1))
        if h == 0:
            args[1], far = lax.optimization_barrier((args[1], far))
    got = []
    for h, (_, b, _, _) in enumerate(axes):
        near += merge((1, 3, 0), h, places[h], factor, args[h])
        near[h], low[h], high[h] = lax.optimization_barrier((near[h], low[h], high[h]))
        t1, t3 = call(
            functools.partial(join_kernel, 64),
            [shape((128, COLS))] * 2,
            [near[h], low[h], high[h]],
            [VM] * 3,
        )
        if h == 0:
            args[1], t1, t3 = lax.optimization_barrier((args[1], t1, t3))
        got += [shift(t1, b, 1), shift(t3, b, -1)]
    keep, send = call(
        cut_kernel,
        [shape((2, 128, 896), F32), shape((2, 128, 896))],
        [ints(xhi), *near, *got],
        [SM] + [VM] * 6,
    )
    send, keep, lat = lax.optimization_barrier((send, keep, lat))
    lat_w = []
    for h in range(2):
        lat_w += [lat[h], shift(lat[h], "core", 1)]
    recv = shift(send, "xhi", 1)

    gain_a = lax.dynamic_index_in_dim(gain_attn.reshape(4, 2, 4, WIDTH), xhi, 1, keepdims=False)
    gain_a = lax.dynamic_index_in_dim(gain_a, y, 1, keepdims=False).reshape(896)
    gains = jnp.stack([gain_a, lax.dynamic_slice_in_dim(gain_attn, z * COLS + xhi * 896, 896)])
    sent = [shape((32, PACK), F32)] + [shape((32, PACK))] * 3
    parts = call(
        latent_kernel,
        sent + sent,
        [ints(core, y, z), keep, recv, gains, *lat_w],
        [SM, VM, VM, VM] + [AN] * 4,
        scratch=[
            pltpu.VMEM((2, 896, PACK), BF),
            pltpu.VMEM((128, PACK), F32),
            pltpu.SemaphoreType.DMA((2, 8)),
        ],
        flops=4 * 128 * 896 * PACK,
        moved=8 * MIB,
        limit=60,
    )
    blocks = []
    for h, (a, _, _, _) in enumerate(axes):
        p = parts[h * 4 : h * 4 + 4]
        blocks += [p[0], *[shift(p[k], a, k) for k in (1, 2, 3)]]
    keep = call(latent_sum_kernel, shape((2, 32, PACK)), blocks, [VM] * 8)
    recv = shift(keep, "xhi", 1)
    cos, sin = rope_tables(seq * TOK + jnp.arange(TOK, dtype=jnp.int32))
    cos, sin, keep = lax.optimization_barrier((cos, sin, keep))
    done = call(
        norm_kernel,
        [shape((32, PACK))] * 2,
        [
            ints(z * 128 + y * 32, HALF + y * 128 + z * 32),
            keep,
            recv,
            gain_query[None],
            gain_kv[None],
            cos,
            sin,
        ],
        [SM] + [VM] * 6,
    )

    ring = [gather_ring(done[h], axes[h][0]) for h in range(2)]
    ring = lax.optimization_barrier(ring)
    rows = [jnp.concatenate(r) for r in ring]
    near = [[shift(rows[h], axes[h][1], d) for d in (-1, 1)] for h in range(2)]
    place = ints(z, y, y, z)
    done = query(((0, 0, 0, 128), (1, 0, 0, 128)), place, query_weight, cos, sin, rows)
    done, near = lax.optimization_barrier((done, near))
    far = [
        [shift(near[h][0][:64], axes[h][1], -1), shift(near[h][1][64:], axes[h][1], 1)]
        for h in range(2)
    ]
    parts = tuple((h, k, 0, 128) for h in range(2) for k in (1, 3))
    done = query(parts, place, query_weight, cos, sin, [*near[0], *near[1]], done)
    done, far = lax.optimization_barrier((done, far))
    parts = tuple((h, 2, at, 64) for h in range(2) for at in (0, 64))
    return query(parts, place, query_weight, cos, sin, [*far[0], *far[1]], done)


def solution(mesh):
    fine = Mesh(mesh.devices.reshape(2, 2, 4, 2, 4), NAMES)
    seq = ("xlo", "core")
    mp = ("z", "xhi", "y")
    placed = (
        P(seq),
        P(seq, mp),
        P(seq, mp),
        P(mp),
        P(mp),
        P(None, mp, None),
        P(),
        P(mp, None),
        P(),
        P(),
        P(None, mp),
    )
    return jax.shard_map(
        per_device,
        mesh=fine,
        in_specs=placed,
        out_specs=(P(seq, mp), P(seq, None), P(seq, None)),
        check_vma=False,
    )
```

```python
import functools

import jax
import jax.numpy as jnp
from jax import lax
from jax.experimental import pallas as pl
from jax.experimental.pallas import tpu as pltpu
from jax.sharding import Mesh, PartitionSpec as P

QL = 1536
KVL = 512
ROPE = 64
NOPE = 128
D = 7168
VOCAB_ROWS = 16160
WIDTH = 224
TOK = 1024
HALF = 512
LAT = QL + KVL + ROPE
PACK = 2176
COLS = 1792

EPSILON = 1e-06
THETA = 10000.0

SIZES = {"xlo": 2, "core": 2, "z": 4, "xhi": 2, "y": 4}
NAMES = ("xlo", "core", "z", "xhi", "y")
BF = jnp.bfloat16
F32 = jnp.float32
MIB = 1 << 20

VM = pl.BlockSpec(memory_space=pltpu.VMEM)
SM = pl.BlockSpec(memory_space=pltpu.SMEM)
AN = pl.BlockSpec(memory_space=pl.ANY)


def shift(x, axis, d):
    n = SIZES[axis]
    return lax.ppermute(x, axis, [(i, (i + d) % n) for i in range(n)])


def gather_ring(x, axis):
    return [x, shift(x, axis, -1), shift(x, axis, 2), shift(x, axis, 1)]


def sum_axis(x, axis):
    if SIZES[axis] == 2:
        return x + shift(x, axis, 1)
    p = gather_ring(x, axis)
    return (p[0] + p[2]) + (p[1] + p[3])


def call(kernel, out_shape, args, specs, scratch=(), flops=0, moved=0, limit=48, **more):
    outs = jax.tree.map(lambda s: VM, out_shape)
    return pl.pallas_call(
        kernel,
        out_shape=out_shape,
        in_specs=specs,
        out_specs=more.pop("out_specs", outs),
        scratch_shapes=list(scratch),
        compiler_params=pltpu.CompilerParams(vmem_limit_bytes=limit * MIB),
        cost_estimate=pl.CostEstimate(flops=flops, bytes_accessed=moved, transcendentals=0),
        **more,
    )(*args)


def shape(dims, dtype=BF):
    return jax.ShapeDtypeStruct(dims, dtype)


STEP = 2048
ROWS = -(-VOCAB_ROWS // STEP) * STEP
NONE = ROWS - 8


def pick_rows(at, rows, picked, outs):
    for part, out in enumerate(outs):

        def some(i, _, part=part):
            base = pl.multiple_of(i * 32, 32)
            for j in range(32):
                picked[pl.ds(base + j, 1), :] = rows[pl.ds(at[part * TOK + base + j], 1), :]
            return 0

        lax.fori_loop(0, TOK // 32, some, 0)
        out[...] = picked[...].astype(BF)


def turn_kernel(at, table_t, out_a, out_b, kept, rows, picked, sem):
    step = pl.program_id(0)
    here = pl.ds(pl.multiple_of(step * STEP, STEP), STEP)
    rows[here, :WIDTH] = table_t[...].astype(F32).T
    rows[here, WIDTH:] = jnp.zeros((STEP, 256 - WIDTH), F32)

    @pl.when(step == pl.num_programs(0) - 1)
    def _():
        rows[pl.ds(NONE, 8), :] = jnp.zeros((8, 256), F32)
        copy = pltpu.make_async_copy(rows, kept, sem)
        copy.start()
        pick_rows(at, rows, picked, (out_a, out_b))
        copy.wait()


def turn(table_t, at):
    out = shape((TOK, 256))
    return pl.pallas_call(
        turn_kernel,
        grid_spec=pltpu.PrefetchScalarGridSpec(
            num_scalar_prefetch=1,
            grid=(ROWS // STEP,),
            in_specs=[pl.BlockSpec((WIDTH, STEP), lambda i, *_: (0, i))],
            out_specs=[pl.BlockSpec((TOK, 256), lambda i, *_: (0, 0))] * 2 + [AN],
            scratch_shapes=[
                pltpu.VMEM((ROWS, 256), F32),
                pltpu.VMEM((TOK, 256), F32),
                pltpu.SemaphoreType.DMA,
            ],
        ),
        out_shape=[out, out, shape((ROWS, 256), F32)],
        compiler_params=pltpu.CompilerParams(vmem_limit_bytes=56 * MIB),
        cost_estimate=pl.CostEstimate(flops=0, bytes_accessed=80 * MIB, transcendentals=0),
    )(at, table_t)


def pick_kernel(at, rows, out_a, out_b, picked):
    pick_rows(at, rows, picked, (out_a, out_b))


def pick(rows, at):
    return call(
        pick_kernel,
        [shape((TOK, 256))] * 2,
        [at, rows],
        [SM, VM],
        scratch=[pltpu.VMEM((TOK, 256), F32)],
        moved=44 * MIB,
    )


def high_low(total):
    high = total.astype(BF).astype(F32)
    return high, total - high


def hidden_kernel(x_t, gain, out):
    x = x_t[...].astype(F32)
    high, low = high_low(jnp.sum(x * x, axis=0, keepdims=True))
    row = lax.broadcasted_iota(jnp.int32, (256 - WIDTH, TOK), 0)
    tail = jnp.where(row == 0, high, jnp.where(row == 1, low, 0.0))
    out[...] = jnp.concatenate([x * gain[...], tail], axis=0).T.astype(BF)


def embed_kernel(own, near, far, gain, hid, out_a, out_b):
    x = own[...].astype(F32) + near[...].astype(F32) + far[...].astype(F32)
    high, low = high_low(jnp.sum(x * x, axis=1, keepdims=True))
    lane = lax.broadcasted_iota(jnp.int32, x.shape, 1)
    x = x * gain[...]
    x = jnp.where(lane == WIDTH, high, jnp.where(lane == WIDTH + 1, low, x)).astype(BF)
    for h, out in enumerate((out_a, out_b)):
        out[:HALF] = hid[h * HALF : (h + 1) * HALF]
        out[HALF:] = x[h * HALF : (h + 1) * HALF]


def square_kernel(*refs):
    args, out, buf, sems = refs[:10], refs[10], refs[11], refs[12]
    lane = lax.broadcasted_iota(jnp.int32, (8, 128), 1)
    take = jnp.where((lane == WIDTH - 128) | (lane == WIDTH - 127), 1.0, 0.0).astype(BF)
    copies = []
    for i, a in enumerate(args):
        rows = a.shape[0]
        c = pltpu.make_async_copy(
            a.at[:, pl.ds(128, 128)], buf.at[i, pl.ds(0, rows), :], sems.at[i]
        )
        c.start()
        copies.append(c)
    for c in copies:
        c.wait()

    def row(x):
        d = lax.dot_general(take, x, (((1,), (1,)), ((), ())), preferred_element_type=F32)
        return d[0:1]

    for h in range(2):
        for m in range(2):
            v = [row(buf[h * 5 + i, pl.ds(m * HALF, HALF), :]) for i in range(3)]
            v.append(row(buf[h * 5 + 3 + m, pl.ds(0, HALF), :]))
            out[pl.ds(h * 2 + m, 1), :] = (v[0] + v[2]) + (v[1] + v[3])


def cut_columns(w, to, dst):
    for xhi in range(2):
        parts = []
        for z in range(4):
            at = (z * 2 + xhi) * 896 + to * WIDTH
            parts.append(w[:, at : at + WIDTH])
        dst[:, xhi * 896 : (xhi + 1) * 896] = jnp.concatenate(parts, axis=1)


def cut_weights_kernel(place, w, out_1, out_2, out_3, wbuf, blocks, sems):
    core, y = place[0], place[1]
    load = pltpu.make_async_copy(w.at[core], wbuf, sems.at[0])
    load.start()
    load.wait()
    for to in range(4):
        pl.when(y != to)(lambda to=to: cut_columns(wbuf, to, blocks.at[to]))
    copies = [
        pltpu.make_async_copy(blocks.at[(y + k) % 4], dst, sems.at[k])
        for k, dst in ((1, out_1), (2, out_2), (3, out_3))
    ]
    for c in copies:
        c.start()
    for c in copies:
        c.wait()


def own_weights_kernel(place, w, own, wbuf, sems):
    copies = [pltpu.make_async_copy(w.at[m], wbuf.at[m], sems.at[m]) for m in range(2)]
    for c in copies:
        c.start()
    for m in range(2):
        copies[m].wait()
        for to in range(4):
            pl.when(place[0] == to)(lambda to=to, m=m: cut_columns(wbuf.at[m], to, own.at[m]))


def load_blocks(core, m, ia, a, rows, wbuf, xbuf, sems):
    copies = []

    def start(src, dst, sem, when=None):
        c = pltpu.make_async_copy(src, dst, sem)
        if when is None:
            c.start()
        else:
            pl.when(when)(lambda: c.start())
        return c

    own = a[10].at[m]
    if a[10].shape[2] != COLS:
        own = own.at[:, pl.ds(pl.multiple_of(ia * COLS, 256), COLS)]
    copies.append(start(own, wbuf.at[pl.ds(0, WIDTH), :], sems.at[0]))
    for i in range(3):
        to = wbuf.at[pl.ds((i + 1) * 256, WIDTH), :]
        start(a[4 + i], to, sems.at[1 + i], core == m)
        copies.append(start(a[7 + i], to, sems.at[1 + i], core != m))
    for k, (src, base) in enumerate(((a[0], m * HALF), (a[1], m * HALF), (a[3], 0), (a[2], m * HALF))):
        done = 0
        for n, (first, count) in enumerate(rows):
            copies.append(
                start(
                    src.at[pl.ds(base + first, count), :],
                    xbuf.at[pl.ds(done, count), pl.ds(k * 256, 256)],
                    sems.at[4 + 4 * n + k],
                )
            )
            done += count
    for k in range(4):
        wbuf[pl.ds(k * 256 + WIDTH, 256 - WIDTH), :] = jnp.zeros((256 - WIDTH, COLS), BF)
    return copies


def merge_kernel(pieces, h, joined, place, fac, *refs):
    a, outs, (wbuf, xbuf, hbuf, fbuf, sems) = refs[:12], refs[12:-5], refs[-5:]
    if joined:
        (low, high), outs = outs[:2], outs[2:]
    rows = [(pl.multiple_of(((place[2] + k) % 4) * 128, 128), 128) for k in pieces]
    copies = [
        load_blocks(
            place[0], m, place[1], [*a[:3], a[3 + m], *a[5:]], rows, wbuf.at[m], xbuf.at[m], sems.at[m]
        )
        for m in range(2)
    ]
    scaled = len(pieces) > 1
    if scaled:
        for n, (at, _) in enumerate(rows):
            fbuf[pl.ds(n * 128, 128), :] = fac[pl.ds(pl.multiple_of(h * HALF + at, 128), 128), :]
        f0, f1 = fbuf[:, 0:1], fbuf[:, 1:2]
    for c in copies[0]:
        c.wait()
    for j in range(7):
        cols = pl.ds(j * 256, 256)
        d = jnp.dot(xbuf[0], wbuf[0, :, cols], preferred_element_type=F32)
        if scaled:
            hbuf[:, cols] = d * f0
        else:
            outs[0][:, cols] = d
    for c in copies[1]:
        c.wait()
    for j in range(7):
        cols = pl.ds(j * 256, 256)
        d = jnp.dot(xbuf[1], wbuf[1, :, cols], preferred_element_type=F32)
        if scaled:
            d = hbuf[:, cols] + d * f1
            if joined:
                outs[0][:64, cols] = (d[:64] + low[:, cols].astype(F32)).astype(BF)
                outs[0][64:, cols] = d[64:128].astype(BF)
                outs[1][:64, cols] = d[128:192].astype(BF)
                outs[1][64:, cols] = (d[192:256] + high[:, cols].astype(F32)).astype(BF)
                outs[2][:, cols] = d[256:]
            else:
                for n in range(3):
                    outs[n][:, cols] = d[n * 128 : n * 128 + 128]
        else:
            outs[1][:, cols] = d


def merge(pieces, h, place, fac, args, arrived=()):
    n = len(pieces)
    outs = [shape((128, COLS), F32)] * (2 if n == 1 else 3)
    if arrived:
        outs[:2] = [shape((128, COLS))] * 2
    return call(
        functools.partial(merge_kernel, pieces, h, bool(arrived)),
        outs,
        [place, fac, *args, *arrived],
        [SM, VM] + [AN] * 12 + [VM] * len(arrived),
        scratch=[
            pltpu.VMEM((2, 1024, COLS), BF),
            pltpu.VMEM((2, n * 128, 1024), BF),
            pltpu.VMEM((n * 128, COLS), F32),
            pltpu.VMEM((n * 128, 2), F32),
            pltpu.SemaphoreType.DMA((2, 4 + 4 * n)),
        ],
        flops=4 * n * 128 * 896 * COLS,
        moved=(16 if n == 1 else 30) * MIB,
        limit=60,
    )


def scale_kernel(place, fac, h_a, e_a, h_b, e_b, low_a, high_a, low_b, high_b):
    for h, (hid, emb, low, high) in enumerate(((h_a, e_a, low_a, high_a), (h_b, e_b, low_b, high_b))):
        at = pl.multiple_of(h * HALF + ((place[h] + 2) % 4) * 128, 128)
        f = fac[pl.ds(at, 128), :]
        total = hid[...] * f[:, 0:1] + emb[...] * f[:, 1:2]
        low[...] = total[:64].astype(BF)
        high[...] = total[64:].astype(BF)


def join_kernel(rows, q1, q3, low, high, t1, t3):
    t1[:rows] = (q1[:rows] + low[...].astype(F32)).astype(BF)
    t1[rows:] = q1[rows:].astype(BF)
    t3[:rows] = q3[:rows].astype(BF)
    t3[rows:] = (q3[rows:] + high[...].astype(F32)).astype(BF)


def cut_kernel(place, q, r1, r3, keep, send):
    xhi = place[0]
    total = q[...] + r1[...].astype(F32) + r3[...].astype(F32)
    keep[...] = jnp.where(xhi == 0, total[:, :896], total[:, 896:])
    send[...] = jnp.where(xhi == 0, total[:, 896:], total[:, :896]).astype(BF)


def split_square(block):
    lane = lax.broadcasted_iota(jnp.int32, block.shape, 1)
    total = jnp.sum(jnp.where((lane == 64) | (lane == 65), block, 0.0), axis=1, keepdims=True)
    high = total.astype(BF).astype(F32)
    block = jnp.where(lane == 64, high, jnp.where(lane == 65, total - high, block))
    return jnp.where(lane > 65, 0.0, block), total


def latent_kernel(place, keep, recv, gain, mine, other, *refs):
    outs, (wbuf, acc, sems) = refs[:4], refs[4:]
    core, at_a = place[0], place[1]
    copies = []
    for k in range(4):
        for s, src in enumerate((mine, other)):
            c_at = core if s == 0 else 1 - core
            row = pl.multiple_of((k * 2 + c_at) * 112, 16)
            c = pltpu.make_async_copy(
                src.at[pl.ds(k * 112, 112), :], wbuf.at[pl.ds(row, 112), :], sems.at[k * 2 + s]
            )
            c.start()
            copies.append(c)
    projected = keep[...] + recv[...].astype(F32)
    square = jnp.sum(projected * projected, axis=1, keepdims=True)
    scaled = (projected * gain[...]).astype(BF)
    for c in copies:
        c.wait()
    for j in range(8):
        cols = pl.ds(j * 256, 256)
        acc[:, cols] = jnp.dot(scaled, wbuf[:, cols], preferred_element_type=F32)
    last = jnp.dot(scaled, wbuf[:, pl.ds(2048, 128)], preferred_element_type=F32)
    lane = lax.broadcasted_iota(jnp.int32, last.shape, 1)
    last, _ = split_square(jnp.where(lane < 64, last, jnp.where(lane == 64, square, 0.0)))
    acc[:, pl.ds(2048, 128)] = last
    for k in (1, 2, 3):
        at = pl.multiple_of(((at_a + k) % 4) * 32, 32)
        outs[k][...] = acc[pl.ds(at, 32), :].astype(BF)
    outs[0][...] = acc[pl.ds(pl.multiple_of(at_a * 32, 32), 32), :]


def latent_sum_kernel(p0, p1, p2, p3, out):
    total = (p0[...] + p1[...].astype(F32)) + (p2[...].astype(F32) + p3[...].astype(F32))
    out[:, :2048] = total[:, :2048].astype(BF)
    last, _ = split_square(total[:, 2048:])
    out[:, 2048:] = last.astype(BF)


def swap_pairs(block):
    lane = lax.broadcasted_iota(jnp.int32, block.shape, 1)
    ahead = pltpu.roll(block, 96, 1)
    behind = pltpu.roll(block, 32, 1)
    return jnp.where(lane % 64 < 32, ahead, behind)


def norm_kernel(
    place, keep_a, recv_a, keep_b, recv_b, gain_q, gain_kv, cos, sin, out_a, out_b, turn_buf, sems
):
    copies = []
    for h in range(2):
        at = pl.ds(pl.multiple_of(place[h], 32), 32)
        for i, src in enumerate((cos, sin)):
            c = pltpu.make_async_copy(src.at[at, :], turn_buf.at[h, i], sems.at[h, i])
            c.start()
            copies.append(c)
    for c in copies:
        c.wait()
    for h, (keep, recv, out) in enumerate(((keep_a, recv_a, out_a), (keep_b, recv_b, out_b))):
        total = keep[...].astype(F32) + recv[...].astype(F32)
        last, square = split_square(total[:, 2048:])
        total = total[:, :2048] * lax.rsqrt(square / D + EPSILON)
        last = last * lax.rsqrt(square / D + EPSILON)
        q, kv = total[:, :QL], total[:, QL:]
        q = q * lax.rsqrt(jnp.mean(q * q, axis=1, keepdims=True) + EPSILON) * gain_q[...]
        kv = kv * lax.rsqrt(jnp.mean(kv * kv, axis=1, keepdims=True) + EPSILON) * gain_kv[...]
        last = last * turn_buf[h, 0] + swap_pairs(last) * turn_buf[h, 1]
        out[:, :QL] = q.astype(BF)
        out[:, QL:2048] = kv.astype(BF)
        out[:, 2048:] = last.astype(BF)


def query_kernel(parts, given, place, weight, cos, sin, *refs):
    n_parts = len(parts)
    blocks, refs = refs[:n_parts], refs[n_parts + given :]
    queries, kv, rope, cbuf, sbuf, qbuf, rbuf, turn_sems, sems = refs
    tables = [
        pltpu.make_async_copy(src, dst, turn_sems.at[i])
        for i, (src, dst) in enumerate(((cos, cbuf), (sin, sbuf)))
    ]
    for c in tables:
        c.start()
    copies = []
    latents = jnp.concatenate([x[:, :QL] for x in blocks], axis=0)
    products = jnp.dot(latents, weight[...], preferred_element_type=F32)
    for c in tables:
        c.wait()
    done = 0
    for n, ((h, kb, first, rows), x) in enumerate(zip(parts, blocks)):
        product = products[done : done + rows]
        done += rows
        rbuf[n, :rows, :] = x[:, pl.ds(2048, 128)][:, :ROPE]
        at_b, at_a = place[h * 2], place[h * 2 + 1]
        for r in range(rows // 32):
            ka = first // 32 + r
            at = pl.multiple_of(
                h * HALF + ((at_b + kb) % 4) * 128 + ((at_a + ka) % 4) * 32, 32
            )
            here = slice(r * 32, r * 32 + 32)
            p = product[here]
            c, s = cbuf[pl.ds(at, 32), :], sbuf[pl.ds(at, 32), :]
            lane = lax.broadcasted_iota(jnp.int32, c.shape, 1)
            for j in range(6):
                blk = p[:, j * 128 : j * 128 + 128]
                if j % 3 != 0:
                    turned = blk * c + swap_pairs(blk) * s
                    mine = lane < 64 if j % 3 == 1 else lane >= 64
                    blk = jnp.where(mine, turned, blk)
                qbuf[n, here, j * 128 : j * 128 + 128] = blk.astype(BF)
            to, part = pl.ds(at, 32), pl.ds(r * 32, 32)
            for i, (src, dst) in enumerate(
                (
                    (qbuf.at[n, part, :], queries.at[to, :]),
                    (x.at[part, pl.ds(QL, KVL)], kv.at[to, :]),
                    (rbuf.at[n, part, :], rope.at[to, :]),
                )
            ):
                cp = pltpu.make_async_copy(src, dst, sems.at[n, r, i])
                cp.start()
                copies.append(cp)
    for cp in copies:
        cp.wait()


def query(parts, place, weight, cos, sin, blocks, given=()):
    n = len(parts)
    tokens = sum(p[3] for p in parts)
    return call(
        functools.partial(query_kernel, parts, len(given)),
        [shape((TOK, 768)), shape((TOK, KVL)), shape((TOK, ROPE))],
        [place, weight, cos, sin, *blocks, *given],
        [SM, VM, AN, AN] + [VM] * n + [AN] * len(given),
        out_specs=[AN] * 3,
        scratch=[
            pltpu.VMEM((TOK, 128), F32),
            pltpu.VMEM((TOK, 128), F32),
            pltpu.VMEM((n, 128, 768), BF),
            pltpu.VMEM((n, 128, ROPE), BF),
            pltpu.SemaphoreType.DMA((2,)),
            pltpu.SemaphoreType.DMA((n, 4, 3)),
        ],
        flops=2 * tokens * QL * 768,
        moved=6 * MIB,
        limit=60,
        input_output_aliases={4 + n + i: i for i in range(len(given))},
    )


def rope_tables(positions):
    lane = jnp.arange(128, dtype=jnp.int32)
    exponent = (lane % 32).astype(F32) * (2.0 / ROPE)
    angles = positions.astype(F32)[:, None] * jnp.power(THETA, -exponent)
    sign = jnp.where(lane % 64 < 32, -1.0, 1.0).astype(F32)
    return jnp.cos(angles), jnp.sin(angles) * sign


def per_device(
    next_ids,
    hidden,
    table,
    gain_hidden,
    gain_embed,
    proj_weight,
    gain_attn,
    latent_weight,
    gain_query,
    gain_kv,
    query_weight,
):
    xlo, core, z, xhi, y = (lax.axis_index(n).astype(jnp.int32) for n in NAMES)
    seq = xlo * 2 + core
    axes = (("y", "z", y, z), ("z", "y", z, y))

    def ints(*v):
        return jnp.stack(v).astype(jnp.int32)

    def weight(m, k, ia):
        return lax.dynamic_slice(proj_weight, (m, 0, ((ia + k) % 4) * COLS), (1, WIDTH, COLS))[0]

    cut_a = call(
        cut_weights_kernel,
        [shape((WIDTH, COLS))] * 3,
        [ints(core, y), proj_weight],
        [SM, AN],
        out_specs=[AN] * 3,
        scratch=[
            pltpu.VMEM((WIDTH, D), BF),
            pltpu.VMEM((4, WIDTH, COLS), BF),
            pltpu.SemaphoreType.DMA((4,)),
        ],
        moved=8 * MIB,
        limit=60,
    )
    cut = [cut_a, [weight(core, k, z) for k in (1, 2, 3)]]

    lat_half = lax.dynamic_slice_in_dim(latent_weight, core * 112, 112, 0)
    lat_half = jnp.pad(lat_half, ((0, 0), (0, PACK - LAT)))

    near_ids = jnp.concatenate([next_ids, shift(next_ids, "core", 1)])
    far_ids = shift(near_ids, "xlo", 1)
    at = jnp.concatenate([far_ids, near_ids]) - seq * VOCAB_ROWS
    at = jnp.where((at >= 0) & (at < VOCAB_ROWS), at, NONE)

    rows, cut, lat_half = lax.optimization_barrier((table.T, cut, lat_half))
    step_3 = [shift(cut[h][0], axes[h][0], 1) for h in range(2)]
    step_1 = [shift(cut[h][2], axes[h][0], -1) for h in range(2)]
    keep, send, rows = turn(rows, at[: 2 * TOK])
    embed_near = keep + shift(send, "core", 1)
    embed_near, step_1, step_3, cut, rows, hidden, lat_half = lax.optimization_barrier(
        (embed_near, step_1, step_3, cut, rows, hidden, lat_half)
    )
    embed_far = shift(embed_near, "xlo", 1)
    step_2 = [shift(cut[h][1], axes[h][0], 2) for h in range(2)]
    keep, send = pick(rows, at[2 * TOK :])
    keep, send, embed_far, step_1, step_3 = lax.optimization_barrier(
        (keep, send, embed_far, step_1, step_3)
    )
    got = shift(send, "core", 1)
    hidden_g = call(
        hidden_kernel, shape((TOK, 256)), [hidden.T, gain_hidden[:, None]], [VM, VM]
    )
    other_1 = [shift(m, "core", 1) for m in step_1]
    other_3 = [shift(m, "core", 1) for m in step_3]
    keep, got, embed_far, step_2, hidden_g, other_1, other_3 = lax.optimization_barrier(
        (keep, got, embed_far, step_2, hidden_g, other_1, other_3)
    )
    gain = jnp.pad(gain_embed, (0, 256 - WIDTH))[None]
    block = call(
        embed_kernel, [shape((TOK, 256))] * 2, [keep, got, embed_far, gain, hidden_g], [VM] * 5
    )

    next_1 = [shift(block[h], axes[h][0], -1) for h in range(2)]
    next_3 = [shift(block[h], axes[h][0], 1) for h in range(2)]
    cos, sin = rope_tables(seq * TOK + jnp.arange(TOK, dtype=jnp.int32))
    own_place, proj_weight, block = lax.optimization_barrier((ints(y), proj_weight, block))
    own_a = call(
        own_weights_kernel,
        shape((2, WIDTH, COLS)),
        [own_place, proj_weight],
        [SM, AN],
        scratch=[pltpu.VMEM((2, WIDTH, D), BF), pltpu.SemaphoreType.DMA((2,))],
        moved=9 * MIB,
        limit=60,
    )
    next_1, next_3, cos, sin, own_a = lax.optimization_barrier((next_1, next_3, cos, sin, own_a))
    own = [own_a, proj_weight]
    hidden_2 = [shift(next_1[h][:HALF], axes[h][0], -1) for h in range(2)]
    embed_2 = [shift(next_3[h][HALF:], axes[h][0], 1) for h in range(2)]
    hidden_2, embed_2, lat_half = lax.optimization_barrier((hidden_2, embed_2, lat_half))
    lat = [lax.all_gather(lat_half, b, axis=0, tiled=True) for _, b, _, _ in axes]
    other_2 = [shift(m, "core", 1) for m in step_2]
    moved = []
    for h in range(2):
        mine, other = [step_1[h], step_2[h], step_3[h]], [other_1[h], other_2[h], other_3[h]]
        moved.append([*mine, *other, own[h]])

    args = []
    for h in range(2):
        args += [block[h], next_1[h], next_3[h], hidden_2[h], embed_2[h]]
    squares = call(
        square_kernel,
        shape((4, HALF), F32),
        args,
        [AN] * 10,
        scratch=[pltpu.VMEM((10, TOK, 128), BF), pltpu.SemaphoreType.DMA((10,))],
        limit=60,
    )
    squares = [squares[:2], squares[2:]]
    args, places = [], []
    for h, (_, _, ia, ib) in enumerate(axes):
        args.append([block[h], next_1[h], next_3[h], hidden_2[h], embed_2[h], *moved[h]])
        places.append(ints(core, ia, ib))
    far = []
    unused = jnp.zeros((8, 128), F32)
    for h in range(2):
        got = [shift(s, axes[i][1], h + 1) for i, s in enumerate(squares)]
        far.append(merge((2,), h, places[h], unused, args[h]))
        squares, got, far, args = lax.optimization_barrier((squares, got, far, args))
        squares = [s + g for s, g in zip(squares, got)]
    squares = sum_axis(jnp.concatenate(squares, axis=1), "xhi")
    factor = lax.rsqrt(squares / D + EPSILON).T

    halves = call(
        scale_kernel,
        [shape((64, COLS))] * 4,
        [ints(z, y), factor, *far[0], *far[1]],
        [SM] + [VM] * 5,
    )
    low, high, near = [], [], []
    for h, (_, b, _, _) in enumerate(axes):
        low.append(shift(halves[h * 2], b, 1))
        high.append(shift(halves[h * 2 + 1], b, -1))
    gain_a = lax.dynamic_index_in_dim(gain_attn.reshape(4, 2, 4, WIDTH), xhi, 1, keepdims=False)
    gain_a = lax.dynamic_index_in_dim(gain_a, y, 1, keepdims=False).reshape(1, 896)
    gain_b = lax.dynamic_slice_in_dim(gain_attn, z * COLS + xhi * 896, 896)[None]
    gains = (gain_a, gain_b)
    barrier = lax.optimization_barrier

    def send_on(h, t):
        b = axes[h][1]
        return [shift(t[0], b, 1), shift(t[1], b, -1)]

    def cut_half(h, got):
        return call(
            cut_kernel,
            [shape((128, 896), F32), shape((128, 896))],
            [ints(xhi), near[h][2], *got],
            [SM] + [VM] * 3,
        )

    def latent_half(h, keep, recv):
        return call(
            latent_kernel,
            [shape((32, PACK), F32)] + [shape((32, PACK))] * 3,
            [ints(core, axes[h][2]), keep, recv, gains[h], *lat_w[h]],
            [SM] + [VM] * 3 + [AN] * 2,
            scratch=[
                pltpu.VMEM((896, PACK), BF),
                pltpu.VMEM((128, PACK), F32),
                pltpu.SemaphoreType.DMA((8,)),
            ],
            flops=2 * 128 * 896 * PACK,
            moved=4 * MIB,
            limit=60,
        )

    def sum_half(blocks):
        return call(latent_sum_kernel, shape((32, PACK)), blocks, [VM] * 4)

    def spread(h, parts):
        return [shift(parts[k], axes[h][0], k) for k in (1, 2, 3)]

    near.append(merge((1, 3, 0), 0, places[0], factor, args[0]))
    near[0], low[0], high[0] = barrier((near[0], low[0], high[0]))
    t_a = call(
        functools.partial(join_kernel, 64),
        [shape((128, COLS))] * 2,
        [*near[0][:2], low[0], high[0]],
        [VM] * 4,
    )
    t_a, args[1] = barrier((t_a, args[1]))
    got_a = send_on(0, t_a)
    near.append(merge((1, 3, 0), 1, places[1], factor, args[1], (low[1], high[1])))
    got_a, near[1], lat = barrier((got_a, near[1], lat))
    t_b = near[1][:2]
    got_b = send_on(1, t_b)
    keep_a, send_a = cut_half(0, got_a)
    lat_w = [[w, shift(w, "core", 1)] for w in lat]
    recv_a = shift(send_a, "xhi", 1)
    got_b, recv_a, lat_w = barrier((got_b, recv_a, lat_w))
    keep_b, send_b = cut_half(1, got_b)
    recv_a, send_b = barrier((recv_a, send_b))
    recv_b = shift(send_b, "xhi", 1)
    parts_a = latent_half(0, keep_a, recv_a)
    recv_b, parts_a = barrier((recv_b, parts_a))
    blocks_a = spread(0, parts_a)
    parts_b = latent_half(1, keep_b, recv_b)
    blocks_a, parts_b = barrier((blocks_a, parts_b))
    blocks_b = spread(1, parts_b)
    keep_a = sum_half([parts_a[0], *blocks_a])
    recv_a = shift(keep_a, "xhi", 1)
    blocks_b, recv_a = barrier((blocks_b, recv_a))
    keep_b = sum_half([parts_b[0], *blocks_b])
    recv_b = shift(keep_b, "xhi", 1)
    done = call(
        norm_kernel,
        [shape((32, PACK))] * 2,
        [
            ints(z * 128 + y * 32, HALF + y * 128 + z * 32),
            keep_a,
            recv_a,
            keep_b,
            recv_b,
            gain_query[None],
            gain_kv[None],
            cos,
            sin,
        ],
        [SM] + [VM] * 6 + [AN] * 2,
        scratch=[pltpu.VMEM((2, 2, 32, 128), F32), pltpu.SemaphoreType.DMA((2, 2))],
        limit=60,
    )

    ring = [gather_ring(done[h], axes[h][0]) for h in range(2)]
    ring = lax.optimization_barrier(ring)
    rows = [jnp.concatenate(r) for r in ring]
    near = [[shift(rows[h], axes[h][1], d) for d in (-1, 1)] for h in range(2)]
    place = ints(z, y, y, z)
    done = query(((0, 0, 0, 128), (1, 0, 0, 128)), place, query_weight, cos, sin, rows)
    done, near = lax.optimization_barrier((done, near))
    far = [
        [shift(near[h][0][:64], axes[h][1], -1), shift(near[h][1][64:], axes[h][1], 1)]
        for h in range(2)
    ]
    parts = tuple((h, k, 0, 128) for h in range(2) for k in (1, 3))
    done = query(parts, place, query_weight, cos, sin, [*near[0], *near[1]], done)
    done, far = lax.optimization_barrier((done, far))
    parts = tuple((h, 2, at, 64) for h in range(2) for at in (0, 64))
    return query(parts, place, query_weight, cos, sin, [*far[0], *far[1]], done)


def solution(mesh):
    fine = Mesh(mesh.devices.reshape(2, 2, 4, 2, 4), NAMES)
    seq = ("xlo", "core")
    mp = ("z", "xhi", "y")
    placed = (
        P(seq),
        P(seq, mp),
        P(seq, mp),
        P(mp),
        P(mp),
        P(None, mp, None),
        P(),
        P(mp, None),
        P(),
        P(),
        P(None, mp),
    )
    return jax.shard_map(
        per_device,
        mesh=fine,
        in_specs=placed,
        out_specs=(P(seq, mp), P(seq, None), P(seq, None)),
        check_vma=False,
    )
```

```python
import functools

import jax
import jax.numpy as jnp
from jax import lax
from jax.experimental import pallas as pl
from jax.experimental.pallas import tpu as pltpu
from jax.sharding import Mesh, PartitionSpec as P

QL = 1536
KVL = 512
ROPE = 64
NOPE = 128
D = 7168
VOCAB_ROWS = 16160
WIDTH = 224
TOK = 1024
HALF = 512
LAT = QL + KVL + ROPE
PACK = 2176
COLS = 1792

EPSILON = 1e-06
THETA = 10000.0

SIZES = {"xlo": 2, "core": 2, "z": 4, "xhi": 2, "y": 4}
NAMES = ("xlo", "core", "z", "xhi", "y")
BF = jnp.bfloat16
F32 = jnp.float32
MIB = 1 << 20

VM = pl.BlockSpec(memory_space=pltpu.VMEM)
SM = pl.BlockSpec(memory_space=pltpu.SMEM)
AN = pl.BlockSpec(memory_space=pl.ANY)


def shift(x, axis, d):
    n = SIZES[axis]
    return lax.ppermute(x, axis, [(i, (i + d) % n) for i in range(n)])


def gather_ring(x, axis):
    return [x, shift(x, axis, -1), shift(x, axis, 2), shift(x, axis, 1)]


def sum_axis(x, axis):
    if SIZES[axis] == 2:
        return x + shift(x, axis, 1)
    p = gather_ring(x, axis)
    return (p[0] + p[2]) + (p[1] + p[3])


def call(kernel, out_shape, args, specs, scratch=(), flops=0, moved=0, limit=48, **more):
    outs = jax.tree.map(lambda s: VM, out_shape)
    return pl.pallas_call(
        kernel,
        out_shape=out_shape,
        in_specs=specs,
        out_specs=more.pop("out_specs", outs),
        scratch_shapes=list(scratch),
        compiler_params=pltpu.CompilerParams(vmem_limit_bytes=limit * MIB),
        cost_estimate=pl.CostEstimate(flops=flops, bytes_accessed=moved, transcendentals=0),
        **more,
    )(*args)


def shape(dims, dtype=BF):
    return jax.ShapeDtypeStruct(dims, dtype)


STEP = 2048
ROWS = -(-VOCAB_ROWS // STEP) * STEP
NONE = ROWS - 8


def pick_rows(at, rows, picked, outs):
    for part, out in enumerate(outs):

        def some(i, _, part=part):
            base = pl.multiple_of(i * 32, 32)
            for j in range(32):
                picked[pl.ds(base + j, 1), :] = rows[pl.ds(at[part * TOK + base + j], 1), :]
            return 0

        lax.fori_loop(0, TOK // 32, some, 0)
        out[...] = picked[...].astype(BF)


def turn_kernel(at, table_t, out_a, out_b, kept, rows, picked, sem):
    step = pl.program_id(0)
    here = pl.ds(pl.multiple_of(step * STEP, STEP), STEP)
    rows[here, :WIDTH] = table_t[...].astype(F32).T
    rows[here, WIDTH:] = jnp.zeros((STEP, 256 - WIDTH), F32)

    @pl.when(step == pl.num_programs(0) - 1)
    def _():
        rows[pl.ds(NONE, 8), :] = jnp.zeros((8, 256), F32)
        copy = pltpu.make_async_copy(rows, kept, sem)
        copy.start()
        pick_rows(at, rows, picked, (out_a, out_b))
        copy.wait()


def turn(table_t, at):
    out = shape((TOK, 256))
    return pl.pallas_call(
        turn_kernel,
        grid_spec=pltpu.PrefetchScalarGridSpec(
            num_scalar_prefetch=1,
            grid=(ROWS // STEP,),
            in_specs=[pl.BlockSpec((WIDTH, STEP), lambda i, *_: (0, i))],
            out_specs=[pl.BlockSpec((TOK, 256), lambda i, *_: (0, 0))] * 2 + [AN],
            scratch_shapes=[
                pltpu.VMEM((ROWS, 256), F32),
                pltpu.VMEM((TOK, 256), F32),
                pltpu.SemaphoreType.DMA,
            ],
        ),
        out_shape=[out, out, shape((ROWS, 256), F32)],
        compiler_params=pltpu.CompilerParams(vmem_limit_bytes=56 * MIB),
        cost_estimate=pl.CostEstimate(flops=0, bytes_accessed=80 * MIB, transcendentals=0),
    )(at, table_t)


def pick_kernel(at, rows, out_a, out_b, picked):
    pick_rows(at, rows, picked, (out_a, out_b))


def pick(rows, at):
    return call(
        pick_kernel,
        [shape((TOK, 256))] * 2,
        [at, rows],
        [SM, VM],
        scratch=[pltpu.VMEM((TOK, 256), F32)],
        moved=44 * MIB,
    )


def high_low(total):
    high = total.astype(BF).astype(F32)
    return high, total - high


def hidden_kernel(x_t, gain, out):
    x = x_t[...].astype(F32)
    high, low = high_low(jnp.sum(x * x, axis=0, keepdims=True))
    row = lax.broadcasted_iota(jnp.int32, (256 - WIDTH, TOK), 0)
    tail = jnp.where(row == 0, high, jnp.where(row == 1, low, 0.0))
    out[...] = jnp.concatenate([x * gain[...], tail], axis=0).T.astype(BF)


def embed_kernel(own, near, far, gain, hid, out_a, out_b):
    x = own[...].astype(F32) + near[...].astype(F32) + far[...].astype(F32)
    high, low = high_low(jnp.sum(x * x, axis=1, keepdims=True))
    lane = lax.broadcasted_iota(jnp.int32, x.shape, 1)
    x = x * gain[...]
    x = jnp.where(lane == WIDTH, high, jnp.where(lane == WIDTH + 1, low, x)).astype(BF)
    for h, out in enumerate((out_a, out_b)):
        out[:HALF] = hid[h * HALF : (h + 1) * HALF]
        out[HALF:] = x[h * HALF : (h + 1) * HALF]


def square_kernel(*refs):
    args, out, buf, sems = refs[:10], refs[10], refs[11], refs[12]
    lane = lax.broadcasted_iota(jnp.int32, (8, 128), 1)
    take = jnp.where((lane == WIDTH - 128) | (lane == WIDTH - 127), 1.0, 0.0).astype(BF)
    copies = []
    for i, a in enumerate(args):
        rows = a.shape[0]
        c = pltpu.make_async_copy(
            a.at[:, pl.ds(128, 128)], buf.at[i, pl.ds(0, rows), :], sems.at[i]
        )
        c.start()
        copies.append(c)
    for c in copies:
        c.wait()

    def row(x):
        d = lax.dot_general(take, x, (((1,), (1,)), ((), ())), preferred_element_type=F32)
        return d[0:1]

    for h in range(2):
        for m in range(2):
            v = [row(buf[h * 5 + i, pl.ds(m * HALF, HALF), :]) for i in range(3)]
            v.append(row(buf[h * 5 + 3 + m, pl.ds(0, HALF), :]))
            out[pl.ds(h * 2 + m, 1), :] = (v[0] + v[2]) + (v[1] + v[3])


def cut_columns(w, to, dst):
    for xhi in range(2):
        parts = []
        for z in range(4):
            at = (z * 2 + xhi) * 896 + to * WIDTH
            parts.append(w[:, at : at + WIDTH])
        dst[:, xhi * 896 : (xhi + 1) * 896] = jnp.concatenate(parts, axis=1)


def cut_weights_kernel(place, w, out_1, out_2, out_3, out_4, out_5, out_6, wbuf, blocks, sems):
    core, y, z = place[0], place[1], place[2]
    load = pltpu.make_async_copy(w.at[core], wbuf, sems.at[0])
    load.start()
    load.wait()
    whole = []
    for k, dst in ((1, out_4), (2, out_5), (3, out_6)):
        cols = pl.ds(pl.multiple_of(((z + k) % 4) * COLS, 256), COLS)
        whole.append(pltpu.make_async_copy(wbuf.at[:, cols], dst, sems.at[3 + k]))
        whole[-1].start()
    for to in range(4):
        pl.when(y != to)(lambda to=to: cut_columns(wbuf, to, blocks.at[to]))
    copies = [
        pltpu.make_async_copy(blocks.at[(y + k) % 4], dst, sems.at[k])
        for k, dst in ((1, out_1), (2, out_2), (3, out_3))
    ]
    for c in copies:
        c.start()
    for c in whole + copies:
        c.wait()


def own_weights_kernel(place, w, own, wbuf, sems):
    copies = [pltpu.make_async_copy(w.at[m], wbuf.at[m], sems.at[m]) for m in range(2)]
    for c in copies:
        c.start()
    for m in range(2):
        copies[m].wait()
        for to in range(4):
            pl.when(place[0] == to)(lambda to=to, m=m: cut_columns(wbuf.at[m], to, own.at[m]))


def load_blocks(core, m, ia, a, rows, wbuf, xbuf, sems):
    copies = []

    def start(src, dst, sem, when=None):
        c = pltpu.make_async_copy(src, dst, sem)
        if when is None:
            c.start()
        else:
            pl.when(when)(lambda: c.start())
        return c

    own = a[10].at[m]
    if a[10].shape[2] != COLS:
        own = own.at[:, pl.ds(pl.multiple_of(ia * COLS, 256), COLS)]
    copies.append(start(own, wbuf.at[pl.ds(0, WIDTH), :], sems.at[0]))
    for i in range(3):
        to = wbuf.at[pl.ds((i + 1) * 256, WIDTH), :]
        start(a[4 + i], to, sems.at[1 + i], core == m)
        copies.append(start(a[7 + i], to, sems.at[1 + i], core != m))
    for k, (src, base) in enumerate(((a[0], m * HALF), (a[1], m * HALF), (a[3], 0), (a[2], m * HALF))):
        done = 0
        for n, (first, count) in enumerate(rows):
            copies.append(
                start(
                    src.at[pl.ds(base + first, count), :],
                    xbuf.at[pl.ds(done, count), pl.ds(k * 256, 256)],
                    sems.at[4 + 4 * n + k],
                )
            )
            done += count
    for k in range(4):
        wbuf[pl.ds(k * 256 + WIDTH, 256 - WIDTH), :] = jnp.zeros((256 - WIDTH, COLS), BF)
    return copies


def merge_kernel(pieces, h, joined, place, fac, *refs):
    a, outs, (wbuf, xbuf, hbuf, fbuf, sems) = refs[:12], refs[12:-5], refs[-5:]
    if joined:
        (low, high), outs = outs[:2], outs[2:]
    rows = [(pl.multiple_of(((place[2] + k) % 4) * 128, 128), 128) for k in pieces]
    copies = [
        load_blocks(
            place[0], m, place[1], [*a[:3], a[3 + m], *a[5:]], rows, wbuf.at[m], xbuf.at[m], sems.at[m]
        )
        for m in range(2)
    ]
    scaled = len(pieces) > 1
    if scaled:
        for n, (at, _) in enumerate(rows):
            fbuf[pl.ds(n * 128, 128), :] = fac[pl.ds(pl.multiple_of(h * HALF + at, 128), 128), :]
        f0, f1 = fbuf[:, 0:1], fbuf[:, 1:2]
    for c in copies[0]:
        c.wait()
    for j in range(7):
        cols = pl.ds(j * 256, 256)
        d = jnp.dot(xbuf[0], wbuf[0, :, cols], preferred_element_type=F32)
        if scaled:
            hbuf[:, cols] = d * f0
        else:
            outs[0][:, cols] = d
    for c in copies[1]:
        c.wait()
    for j in range(7):
        cols = pl.ds(j * 256, 256)
        d = jnp.dot(xbuf[1], wbuf[1, :, cols], preferred_element_type=F32)
        if scaled:
            d = hbuf[:, cols] + d * f1
            if joined:
                outs[0][:64, cols] = (d[:64] + low[:, cols].astype(F32)).astype(BF)
                outs[0][64:, cols] = d[64:128].astype(BF)
                outs[1][:64, cols] = d[128:192].astype(BF)
                outs[1][64:, cols] = (d[192:256] + high[:, cols].astype(F32)).astype(BF)
                outs[2][:, cols] = d[256:]
            else:
                for n in range(3):
                    outs[n][:, cols] = d[n * 128 : n * 128 + 128]
        else:
            outs[1][:, cols] = d


def merge(pieces, h, place, fac, args, arrived=()):
    n = len(pieces)
    outs = [shape((128, COLS), F32)] * (2 if n == 1 else 3)
    if arrived:
        outs[:2] = [shape((128, COLS))] * 2
    return call(
        functools.partial(merge_kernel, pieces, h, bool(arrived)),
        outs,
        [place, fac, *args, *arrived],
        [SM, VM] + [AN] * 12 + [VM] * len(arrived),
        scratch=[
            pltpu.VMEM((2, 1024, COLS), BF),
            pltpu.VMEM((2, n * 128, 1024), BF),
            pltpu.VMEM((n * 128, COLS), F32),
            pltpu.VMEM((n * 128, 2), F32),
            pltpu.SemaphoreType.DMA((2, 4 + 4 * n)),
        ],
        flops=4 * n * 128 * 896 * COLS,
        moved=(16 if n == 1 else 30) * MIB,
        limit=60,
    )


def fetch(srcs, buf, sems):
    copies = [pltpu.make_async_copy(a, buf.at[i], sems.at[i]) for i, a in enumerate(srcs)]
    for c in copies:
        c.start()
    return copies


def scale_kernel(place, fac, h_a, e_a, h_b, e_b, low_a, high_a, low_b, high_b, buf, sems):
    copies = fetch((h_a, e_a, h_b, e_b), buf, sems)
    for h, (low, high) in enumerate(((low_a, high_a), (low_b, high_b))):
        copies[h * 2].wait()
        copies[h * 2 + 1].wait()
        hid, emb = buf.at[h * 2], buf.at[h * 2 + 1]
        at = pl.multiple_of(h * HALF + ((place[h] + 2) % 4) * 128, 128)
        f = fac[pl.ds(at, 128), :]
        total = hid[...] * f[:, 0:1] + emb[...] * f[:, 1:2]
        low[...] = total[:64].astype(BF)
        high[...] = total[64:].astype(BF)


def join_kernel(rows, q1, q3, low, high, t1, t3, buf, sems):
    copies = fetch((q1, q3), buf, sems)
    copies[0].wait()
    t1[:rows] = (buf[0, :rows] + low[...].astype(F32)).astype(BF)
    t1[rows:] = buf[0, rows:].astype(BF)
    copies[1].wait()
    t3[:rows] = buf[1, :rows].astype(BF)
    t3[rows:] = (buf[1, rows:] + high[...].astype(F32)).astype(BF)


def cut_kernel(place, q, r1, r3, keep, send):
    xhi = place[0]
    total = q[...] + r1[...].astype(F32) + r3[...].astype(F32)
    keep[...] = jnp.where(xhi == 0, total[:, :896], total[:, 896:])
    send[...] = jnp.where(xhi == 0, total[:, 896:], total[:, :896]).astype(BF)


def split_square(block):
    lane = lax.broadcasted_iota(jnp.int32, block.shape, 1)
    total = jnp.sum(jnp.where((lane == 64) | (lane == 65), block, 0.0), axis=1, keepdims=True)
    high = total.astype(BF).astype(F32)
    block = jnp.where(lane == 64, high, jnp.where(lane == 65, total - high, block))
    return jnp.where(lane > 65, 0.0, block), total


def latent_kernel(place, keep, recv, gain, mine, other, *refs):
    outs, (wbuf, acc, sems) = refs[:4], refs[4:]
    core, at_a = place[0], place[1]
    copies = []
    for k in range(4):
        for s, src in enumerate((mine, other)):
            c_at = core if s == 0 else 1 - core
            row = pl.multiple_of((k * 2 + c_at) * 112, 16)
            c = pltpu.make_async_copy(
                src.at[pl.ds(k * 112, 112), :], wbuf.at[pl.ds(row, 112), :], sems.at[k * 2 + s]
            )
            c.start()
            copies.append(c)
    projected = keep[...] + recv[...].astype(F32)
    square = jnp.sum(projected * projected, axis=1, keepdims=True)
    scaled = (projected * gain[...]).astype(BF)
    for c in copies:
        c.wait()
    for j in range(8):
        cols = pl.ds(j * 256, 256)
        acc[:, cols] = jnp.dot(scaled, wbuf[:, cols], preferred_element_type=F32)
    last = jnp.dot(scaled, wbuf[:, pl.ds(2048, 128)], preferred_element_type=F32)
    lane = lax.broadcasted_iota(jnp.int32, last.shape, 1)
    last, _ = split_square(jnp.where(lane < 64, last, jnp.where(lane == 64, square, 0.0)))
    acc[:, pl.ds(2048, 128)] = last
    for k in (1, 2, 3):
        at = pl.multiple_of(((at_a + k) % 4) * 32, 32)
        outs[k][...] = acc[pl.ds(at, 32), :].astype(BF)
    outs[0][...] = acc[pl.ds(pl.multiple_of(at_a * 32, 32), 32), :]


def latent_sum_kernel(p0, p1, p2, p3, out):
    total = (p0[...] + p1[...].astype(F32)) + (p2[...].astype(F32) + p3[...].astype(F32))
    out[:, :2048] = total[:, :2048].astype(BF)
    last, _ = split_square(total[:, 2048:])
    out[:, 2048:] = last.astype(BF)


def swap_pairs(block):
    lane = lax.broadcasted_iota(jnp.int32, block.shape, 1)
    ahead = pltpu.roll(block, 96, 1)
    behind = pltpu.roll(block, 32, 1)
    return jnp.where(lane % 64 < 32, ahead, behind)


def norm_kernel(
    place, keep_a, recv_a, keep_b, recv_b, gain_q, gain_kv, cos, sin, out_a, out_b, turn_buf, sems
):
    copies = []
    for h in range(2):
        at = pl.ds(pl.multiple_of(place[h], 32), 32)
        for i, src in enumerate((cos, sin)):
            c = pltpu.make_async_copy(src.at[at, :], turn_buf.at[h, i], sems.at[h, i])
            c.start()
            copies.append(c)
    for c in copies:
        c.wait()
    for h, (keep, recv, out) in enumerate(((keep_a, recv_a, out_a), (keep_b, recv_b, out_b))):
        total = keep[...].astype(F32) + recv[...].astype(F32)
        last, square = split_square(total[:, 2048:])
        total = total[:, :2048] * lax.rsqrt(square / D + EPSILON)
        last = last * lax.rsqrt(square / D + EPSILON)
        q, kv = total[:, :QL], total[:, QL:]
        q = q * lax.rsqrt(jnp.mean(q * q, axis=1, keepdims=True) + EPSILON) * gain_q[...]
        kv = kv * lax.rsqrt(jnp.mean(kv * kv, axis=1, keepdims=True) + EPSILON) * gain_kv[...]
        last = last * turn_buf[h, 0] + swap_pairs(last) * turn_buf[h, 1]
        out[:, :QL] = q.astype(BF)
        out[:, QL:2048] = kv.astype(BF)
        out[:, 2048:] = last.astype(BF)


def query_kernel(parts, given, place, weight, cos, sin, *refs):
    n_parts = len(parts)
    blocks, refs = refs[:n_parts], refs[n_parts + given :]
    queries, kv, rope, cbuf, sbuf, qbuf, rbuf, turn_sems, sems = refs
    tables = [
        pltpu.make_async_copy(src, dst, turn_sems.at[i])
        for i, (src, dst) in enumerate(((cos, cbuf), (sin, sbuf)))
    ]
    for c in tables:
        c.start()
    copies = []
    latents = jnp.concatenate([x[:, :QL] for x in blocks], axis=0)
    products = jnp.dot(latents, weight[...], preferred_element_type=F32)
    for c in tables:
        c.wait()
    done = 0
    for n, ((h, kb, first, rows), x) in enumerate(zip(parts, blocks)):
        product = products[done : done + rows]
        done += rows
        rbuf[n, :rows, :] = x[:, pl.ds(2048, 128)][:, :ROPE]
        at_b, at_a = place[h * 2], place[h * 2 + 1]
        for r in range(rows // 32):
            ka = first // 32 + r
            at = pl.multiple_of(
                h * HALF + ((at_b + kb) % 4) * 128 + ((at_a + ka) % 4) * 32, 32
            )
            here = slice(r * 32, r * 32 + 32)
            p = product[here]
            c, s = cbuf[pl.ds(at, 32), :], sbuf[pl.ds(at, 32), :]
            lane = lax.broadcasted_iota(jnp.int32, c.shape, 1)
            for j in range(6):
                blk = p[:, j * 128 : j * 128 + 128]
                if j % 3 != 0:
                    turned = blk * c + swap_pairs(blk) * s
                    mine = lane < 64 if j % 3 == 1 else lane >= 64
                    blk = jnp.where(mine, turned, blk)
                qbuf[n, here, j * 128 : j * 128 + 128] = blk.astype(BF)
            to, part = pl.ds(at, 32), pl.ds(r * 32, 32)
            for i, (src, dst) in enumerate(
                (
                    (qbuf.at[n, part, :], queries.at[to, :]),
                    (x.at[part, pl.ds(QL, KVL)], kv.at[to, :]),
                    (rbuf.at[n, part, :], rope.at[to, :]),
                )
            ):
                cp = pltpu.make_async_copy(src, dst, sems.at[n, r, i])
                cp.start()
                copies.append(cp)
    for cp in copies:
        cp.wait()


def query(parts, place, weight, cos, sin, blocks, given=()):
    n = len(parts)
    tokens = sum(p[3] for p in parts)
    return call(
        functools.partial(query_kernel, parts, len(given)),
        [shape((TOK, 768)), shape((TOK, KVL)), shape((TOK, ROPE))],
        [place, weight, cos, sin, *blocks, *given],
        [SM, VM, AN, AN] + [VM] * n + [AN] * len(given),
        out_specs=[AN] * 3,
        scratch=[
            pltpu.VMEM((TOK, 128), F32),
            pltpu.VMEM((TOK, 128), F32),
            pltpu.VMEM((n, 128, 768), BF),
            pltpu.VMEM((n, 128, ROPE), BF),
            pltpu.SemaphoreType.DMA((2,)),
            pltpu.SemaphoreType.DMA((n, 4, 3)),
        ],
        flops=2 * tokens * QL * 768,
        moved=6 * MIB,
        limit=60,
        input_output_aliases={4 + n + i: i for i in range(len(given))},
    )


def rope_tables(positions):
    lane = jnp.arange(128, dtype=jnp.int32)
    exponent = (lane % 32).astype(F32) * (2.0 / ROPE)
    angles = positions.astype(F32)[:, None] * jnp.power(THETA, -exponent)
    sign = jnp.where(lane % 64 < 32, -1.0, 1.0).astype(F32)
    return jnp.cos(angles), jnp.sin(angles) * sign


def per_device(
    next_ids,
    hidden,
    table,
    gain_hidden,
    gain_embed,
    proj_weight,
    gain_attn,
    latent_weight,
    gain_query,
    gain_kv,
    query_weight,
):
    xlo, core, z, xhi, y = (lax.axis_index(n).astype(jnp.int32) for n in NAMES)
    seq = xlo * 2 + core
    axes = (("y", "z", y, z), ("z", "y", z, y))

    def ints(*v):
        return jnp.stack(v).astype(jnp.int32)

    cut = call(
        cut_weights_kernel,
        [shape((WIDTH, COLS))] * 6,
        [ints(core, y, z), proj_weight],
        [SM, AN],
        out_specs=[AN] * 6,
        scratch=[
            pltpu.VMEM((WIDTH, D), BF),
            pltpu.VMEM((4, WIDTH, COLS), BF),
            pltpu.SemaphoreType.DMA((7,)),
        ],
        moved=8 * MIB,
        limit=60,
    )
    cut = [cut[:3], cut[3:]]

    lat_half = lax.dynamic_slice_in_dim(latent_weight, core * 112, 112, 0)
    lat_half = jnp.pad(lat_half, ((0, 0), (0, PACK - LAT)))

    near_ids = jnp.concatenate([next_ids, shift(next_ids, "core", 1)])
    far_ids = shift(near_ids, "xlo", 1)
    at = jnp.concatenate([far_ids, near_ids]) - seq * VOCAB_ROWS
    at = jnp.where((at >= 0) & (at < VOCAB_ROWS), at, NONE)

    rows, cut, lat_half = lax.optimization_barrier((table.T, cut, lat_half))
    step_3 = [shift(cut[h][0], axes[h][0], 1) for h in range(2)]
    step_1 = [shift(cut[h][2], axes[h][0], -1) for h in range(2)]
    keep, send, rows = turn(rows, at[: 2 * TOK])
    embed_near = keep + shift(send, "core", 1)
    embed_near, step_1, step_3, cut, rows, hidden, lat_half = lax.optimization_barrier(
        (embed_near, step_1, step_3, cut, rows, hidden, lat_half)
    )
    embed_far = shift(embed_near, "xlo", 1)
    step_2 = [shift(cut[h][1], axes[h][0], 2) for h in range(2)]
    keep, send = pick(rows, at[2 * TOK :])
    keep, send, embed_far, step_1, step_3 = lax.optimization_barrier(
        (keep, send, embed_far, step_1, step_3)
    )
    got = shift(send, "core", 1)
    hidden_g = call(
        hidden_kernel, shape((TOK, 256)), [hidden.T, gain_hidden[:, None]], [VM, VM]
    )
    other_1 = [shift(m, "core", 1) for m in step_1]
    other_3 = [shift(m, "core", 1) for m in step_3]
    keep, got, embed_far, step_2, hidden_g, other_1, other_3 = lax.optimization_barrier(
        (keep, got, embed_far, step_2, hidden_g, other_1, other_3)
    )
    gain = jnp.pad(gain_embed, (0, 256 - WIDTH))[None]
    block = call(
        embed_kernel, [shape((TOK, 256))] * 2, [keep, got, embed_far, gain, hidden_g], [VM] * 5
    )

    next_1 = [shift(block[h], axes[h][0], -1) for h in range(2)]
    next_3 = [shift(block[h], axes[h][0], 1) for h in range(2)]
    cos, sin = rope_tables(seq * TOK + jnp.arange(TOK, dtype=jnp.int32))
    own_place, proj_weight, block = lax.optimization_barrier((ints(y), proj_weight, block))
    own_a = call(
        own_weights_kernel,
        shape((2, WIDTH, COLS)),
        [own_place, proj_weight],
        [SM, AN],
        scratch=[pltpu.VMEM((2, WIDTH, D), BF), pltpu.SemaphoreType.DMA((2,))],
        moved=9 * MIB,
        limit=60,
    )
    next_1, next_3, cos, sin, own_a = lax.optimization_barrier((next_1, next_3, cos, sin, own_a))
    own = [own_a, proj_weight]
    hidden_2 = [shift(next_1[h][:HALF], axes[h][0], -1) for h in range(2)]
    embed_2 = [shift(next_3[h][HALF:], axes[h][0], 1) for h in range(2)]
    hidden_2, embed_2, lat_half = lax.optimization_barrier((hidden_2, embed_2, lat_half))
    lat = [lax.all_gather(lat_half, b, axis=0, tiled=True) for _, b, _, _ in axes]
    other_2 = [shift(m, "core", 1) for m in step_2]
    moved = []
    for h in range(2):
        mine, other = [step_1[h], step_2[h], step_3[h]], [other_1[h], other_2[h], other_3[h]]
        moved.append([*mine, *other, own[h]])

    args = []
    for h in range(2):
        args += [block[h], next_1[h], next_3[h], hidden_2[h], embed_2[h]]
    squares = call(
        square_kernel,
        shape((4, HALF), F32),
        args,
        [AN] * 10,
        scratch=[pltpu.VMEM((10, TOK, 128), BF), pltpu.SemaphoreType.DMA((10,))],
        limit=60,
    )
    squares = [squares[:2], squares[2:]]
    args, places = [], []
    for h, (_, _, ia, ib) in enumerate(axes):
        args.append([block[h], next_1[h], next_3[h], hidden_2[h], embed_2[h], *moved[h]])
        places.append(ints(core, ia, ib))
    far = []
    unused = jnp.zeros((8, 128), F32)
    for h in range(2):
        got = [shift(s, axes[i][1], h + 1) for i, s in enumerate(squares)]
        far.append(merge((2,), h, places[h], unused, args[h]))
        squares, got, far, args = lax.optimization_barrier((squares, got, far, args))
        squares = [s + g for s, g in zip(squares, got)]
    squares = sum_axis(jnp.concatenate(squares, axis=1), "xhi")
    factor = lax.rsqrt(squares / D + EPSILON).T

    halves = call(
        scale_kernel,
        [shape((64, COLS))] * 4,
        [ints(z, y), factor, *far[0], *far[1]],
        [SM, VM] + [AN] * 4,
        scratch=[pltpu.VMEM((4, 128, COLS), F32), pltpu.SemaphoreType.DMA((4,))],
        limit=60,
    )
    low, high, near = [], [], []
    for h, (_, b, _, _) in enumerate(axes):
        low.append(shift(halves[h * 2], b, 1))
        high.append(shift(halves[h * 2 + 1], b, -1))
    gain_a = lax.dynamic_index_in_dim(gain_attn.reshape(4, 2, 4, WIDTH), xhi, 1, keepdims=False)
    gain_a = lax.dynamic_index_in_dim(gain_a, y, 1, keepdims=False).reshape(1, 896)
    gain_b = lax.dynamic_slice_in_dim(gain_attn, z * COLS + xhi * 896, 896)[None]
    gains = (gain_a, gain_b)
    barrier = lax.optimization_barrier

    def send_on(h, t):
        b = axes[h][1]
        return [shift(t[0], b, 1), shift(t[1], b, -1)]

    def cut_half(h, got):
        return call(
            cut_kernel,
            [shape((128, 896), F32), shape((128, 896))],
            [ints(xhi), near[h][2], *got],
            [SM] + [VM] * 3,
        )

    def latent_half(h, keep, recv):
        return call(
            latent_kernel,
            [shape((32, PACK), F32)] + [shape((32, PACK))] * 3,
            [ints(core, axes[h][2]), keep, recv, gains[h], *lat_w[h]],
            [SM] + [VM] * 3 + [AN] * 2,
            scratch=[
                pltpu.VMEM((896, PACK), BF),
                pltpu.VMEM((128, PACK), F32),
                pltpu.SemaphoreType.DMA((8,)),
            ],
            flops=2 * 128 * 896 * PACK,
            moved=4 * MIB,
            limit=60,
        )

    def sum_half(blocks):
        return call(latent_sum_kernel, shape((32, PACK)), blocks, [VM] * 4)

    def spread(h, parts):
        return [shift(parts[k], axes[h][0], k) for k in (1, 2, 3)]

    near.append(merge((1, 3, 0), 0, places[0], factor, args[0]))
    near[0], low[0], high[0] = barrier((near[0], low[0], high[0]))
    t_a = call(
        functools.partial(join_kernel, 64),
        [shape((128, COLS))] * 2,
        [*near[0][:2], low[0], high[0]],
        [AN] * 2 + [VM] * 2,
        scratch=[pltpu.VMEM((2, 128, COLS), F32), pltpu.SemaphoreType.DMA((2,))],
        limit=60,
    )
    t_a, args[1] = barrier((t_a, args[1]))
    got_a = send_on(0, t_a)
    near.append(merge((1, 3, 0), 1, places[1], factor, args[1], (low[1], high[1])))
    got_a, near[1], lat = barrier((got_a, near[1], lat))
    t_b = near[1][:2]
    got_b = send_on(1, t_b)
    keep_a, send_a = cut_half(0, got_a)
    lat_w = [[w, shift(w, "core", 1)] for w in lat]
    recv_a = shift(send_a, "xhi", 1)
    got_b, recv_a, lat_w = barrier((got_b, recv_a, lat_w))
    keep_b, send_b = cut_half(1, got_b)
    recv_a, send_b = barrier((recv_a, send_b))
    recv_b = shift(send_b, "xhi", 1)
    parts_a = latent_half(0, keep_a, recv_a)
    recv_b, parts_a = barrier((recv_b, parts_a))
    blocks_a = spread(0, parts_a)
    parts_b = latent_half(1, keep_b, recv_b)
    blocks_a, parts_b = barrier((blocks_a, parts_b))
    blocks_b = spread(1, parts_b)
    keep_a = sum_half([parts_a[0], *blocks_a])
    recv_a = shift(keep_a, "xhi", 1)
    blocks_b, recv_a = barrier((blocks_b, recv_a))
    keep_b = sum_half([parts_b[0], *blocks_b])
    recv_b = shift(keep_b, "xhi", 1)
    done = call(
        norm_kernel,
        [shape((32, PACK))] * 2,
        [
            ints(z * 128 + y * 32, HALF + y * 128 + z * 32),
            keep_a,
            recv_a,
            keep_b,
            recv_b,
            gain_query[None],
            gain_kv[None],
            cos,
            sin,
        ],
        [SM] + [VM] * 6 + [AN] * 2,
        scratch=[pltpu.VMEM((2, 2, 32, 128), F32), pltpu.SemaphoreType.DMA((2, 2))],
        limit=60,
    )

    ring = [gather_ring(done[h], axes[h][0]) for h in range(2)]
    ring = lax.optimization_barrier(ring)
    rows = [jnp.concatenate(r) for r in ring]
    near = [[shift(rows[h], axes[h][1], d) for d in (-1, 1)] for h in range(2)]
    place = ints(z, y, y, z)
    done = query(((0, 0, 0, 128), (1, 0, 0, 128)), place, query_weight, cos, sin, rows)
    done, near = lax.optimization_barrier((done, near))
    far = [
        [shift(near[h][0][:64], axes[h][1], -1), shift(near[h][1][64:], axes[h][1], 1)]
        for h in range(2)
    ]
    parts = tuple((h, k, 0, 128) for h in range(2) for k in (1, 3))
    done = query(parts, place, query_weight, cos, sin, [*near[0], *near[1]], done)
    done, far = lax.optimization_barrier((done, far))
    parts = tuple((h, 2, at, 64) for h in range(2) for at in (0, 64))
    return query(parts, place, query_weight, cos, sin, [*far[0], *far[1]], done)


def solution(mesh):
    fine = Mesh(mesh.devices.reshape(2, 2, 4, 2, 4), NAMES)
    seq = ("xlo", "core")
    mp = ("z", "xhi", "y")
    placed = (
        P(seq),
        P(seq, mp),
        P(seq, mp),
        P(mp),
        P(mp),
        P(None, mp, None),
        P(),
        P(mp, None),
        P(),
        P(),
        P(None, mp),
    )
    return jax.shard_map(
        per_device,
        mesh=fine,
        in_specs=placed,
        out_specs=(P(seq, mp), P(seq, None), P(seq, None)),
        check_vma=False,
    )
```
